32 devices in a mesh: parts: 2 (over y), tensor: 4 (over z), dp: 4 (over x, core).
Axes of the slice: x: 2, y: 2, z: 4, core: 2. Of those that a mesh axis runs over, the one named last changes fastest.
Arguments:
- inputs: bfloat16 [4096, 8192], P(('parts', 'dp'), 'tensor'), parts along dimension 0, may hold values from -6 to 6
- out_grad: bfloat16 [4096, 4, 2048], P(('parts', 'dp'), None, 'tensor'), parts along dimension 0, may hold values from -6 to 6
- gate_pre: bfloat16 [4096, 28672], P(('parts', 'dp'), 'tensor'), parts along dimension 0, may hold values from -8 to 8
- down_weight: bfloat16 [28672, 8192], P('tensor', 'dp'), may hold values from -0.03125 to 0.03125
- proj_in: bfloat16 [8192, 64], P('tensor'), may hold values from -0.0625 to 0.0625
- proj_out: bfloat16 [28672, 64], P('tensor'), may hold values from -0.09375 to 0.09375
- queries: bfloat16 [256, 4096], P('tensor', 'dp'), may hold values from -0.1875 to 0.1875
Outputs:
- scores: float32 [256, 4096], P('tensor', ('parts', 'dp')), parts along dimension 1
The draws below stay inside these ranges and needn't reach their ends.
There are 2 independent parts, one for each index of `parts`. The reference program is written for one: setup_inputs(seed, part) draws one part's arguments, and reference() takes and returns one part's arrays. A program takes and returns all parts, laid end to end along the dimension named above; an argument that names none is the same for every part. Nothing has to cross between parts.
All inputs are finite; a program needn't handle non-finite values.
Results may differ from the reference program's by a relative error of at most 0.0041.
Values may be sent and summed in bfloat16 or wider, within the bound.
No kernel may reach another device: no remote copies, remote signals or barrier semaphores. Data moves between devices by JAX's collectives and lax.ppermute only.
A program may use at most 320 MiB of HBM per device.

```python
import jax
import jax.numpy as jnp

D = 8192
FF = 28672
K = 64
TOKENS = 2048
NQ = 256
N_DP = 4


def level_of(rng, dims, pieces, smallest, high):
    def one(position, parts):
        draws = jax.random.uniform(jax.random.fold_in(jax.random.fold_in(rng, 6), position), (parts,), jnp.float32, smallest / len(pieces), high / len(pieces))
        return jnp.repeat(jnp.exp(draws), dims[position] // parts).reshape((-1,) + (1,) * (len(dims) - position - 1))

    factor_of = one(*pieces[0])
    for cut in pieces[1:]:
        factor_of = factor_of * one(*cut)
    return factor_of


def bell_draw(rng, dims, deviation, reach, shards=(), dtype=jnp.bfloat16):
    entries = deviation * jax.random.normal(rng, dims, jnp.float32)
    if shards:
        entries = entries * level_of(rng, dims, shards, -0.22, 0.18)
    return jnp.clip(entries, -reach, reach).astype(dtype)


def setup_inputs(seed: int = 0, part: int = 0) -> dict:
    splits = jax.random.split(jax.random.key(seed), 8)
    own_keys = jax.random.split(jax.random.fold_in(splits[7], part), 8)
    return {
        "inputs": bell_draw(own_keys[0], (TOKENS, D), 1.0, 6.0, ((0, 4), (1, 4))),
        "out_grad": bell_draw(own_keys[1], (TOKENS, N_DP, D // N_DP), 1.0, 6.0, ((0, 4), (2, 4))),
        "gate_pre": bell_draw(own_keys[2], (TOKENS, FF), 2.0, 8.0, ((0, 4), (1, 4))),
        "down_weight": bell_draw(splits[3], (FF, D), FF ** -0.5, 0.03125, ((0, 4), (1, 4))),
        "proj_in": bell_draw(splits[4], (D, K), D ** -0.5, 0.0625, ((0, 4),)),
        "proj_out": bell_draw(splits[5], (FF, K), (FF // 8) ** -0.5, 0.09375, ((0, 4),)),
        "queries": bell_draw(splits[6], (NQ, K * K), (K * K // 4) ** -0.5, 0.1875, ((0, 4), (1, 4))),
    }


def reference(inputs, out_grad, gate_pre, down_weight, proj_in, proj_out, queries):
    grad_rows = out_grad.reshape(out_grad.shape[0], -1)
    hidden_grad = jnp.dot(grad_rows, down_weight.T, preferred_element_type=jnp.float32)
    gate_value = gate_pre.astype(jnp.float32)
    up_grad = (hidden_grad * jax.nn.silu(gate_value)).astype(jnp.bfloat16)
    grad_proj = jnp.dot(up_grad, proj_out, preferred_element_type=jnp.float32)
    input_proj = jnp.dot(inputs, proj_in, preferred_element_type=jnp.float32)
    features = (input_proj[:, :, None] * grad_proj[:, None, :]).reshape(input_proj.shape[0], -1).astype(jnp.bfloat16)
    return jnp.dot(queries, features.T, preferred_element_type=jnp.float32)
```

```python
import functools

import jax
import jax.numpy as jnp
from jax import lax
from jax.experimental import pallas as pl
from jax.experimental.pallas import tpu as pltpu
from jax.sharding import PartitionSpec as P

LANES = 128
CHUNK = 1024
TILE = 512


def swap(value, axis, size, mask):
    return lax.ppermute(value, axis, [(i, i ^ mask) for i in range(size)])


def project_kernel(shards, grad_ref, gate_ref, weight_ref, proj_ref, out_ref):
    @pl.when(pl.program_id(0) == 0)
    def _():
        out_ref[...] = jnp.zeros_like(out_ref)

    width = grad_ref.shape[2]
    hidden = None
    for shard in range(shards):
        term = lax.dot_general(
            grad_ref[shard],
            weight_ref[:, shard * width : (shard + 1) * width],
            (((1,), (1,)), ((), ())),
            preferred_element_type=jnp.float32,
        )
        hidden = term if hidden is None else hidden + term
    gate = gate_ref[...].astype(jnp.float32)
    up_grad = (hidden * (gate / (1.0 + jnp.exp(-gate)))).astype(jnp.bfloat16)
    out_ref[...] += jnp.dot(up_grad, proj_ref[...], preferred_element_type=jnp.float32)


def project(grad, gate, weight, proj, offset, span, local_gate):
    shards, rows, width = grad.shape
    tile = TILE if span % TILE == 0 else span
    first = offset // tile
    gate_first = first if local_gate else 0
    return pl.pallas_call(
        functools.partial(project_kernel, shards),
        grid=(span // tile,),
        in_specs=[
            pl.BlockSpec((shards, rows, width), lambda i: (0, 0, 0)),
            pl.BlockSpec((rows, tile), lambda i: (0, gate_first + i)),
            pl.BlockSpec((tile, shards * width), lambda i: (first + i, 0)),
            pl.BlockSpec((tile, proj.shape[1]), lambda i: (first + i, 0)),
        ],
        out_specs=pl.BlockSpec((rows, proj.shape[1]), lambda i: (0, 0)),
        out_shape=jax.ShapeDtypeStruct((rows, proj.shape[1]), jnp.float32),
        compiler_params=pltpu.CompilerParams(vmem_limit_bytes=40 * 1024 * 1024),
        cost_estimate=pl.CostEstimate(
            flops=2 * rows * span * (shards * width + 4 * proj.shape[1]),
            bytes_accessed=2 * span * (shards * width + rows),
            transcendentals=rows * span,
        ),
    )(grad, gate, weight, proj)


def sum_over(value, axis, size):
    mask = 1
    while mask < size:
        value = value + swap(value, axis, size, mask)
        mask *= 2
    return value


def on_device(n_dp, n_tensor, inputs, out_grad, gate_pre, down_weight, proj_in, proj_out, queries):
    rows = out_grad.shape[0]
    hidden = gate_pre.shape[1]
    me = lax.axis_index("dp")
    far, near = n_dp // 2, 1

    chunk = CHUNK if hidden % CHUNK == 0 else hidden
    starts = list(range(0, hidden, chunk))

    def gather(block):
        grad = lax.all_gather(block, "tensor", axis=0, tiled=False)
        if block.shape[1] % LANES:
            grad = jnp.swapaxes(grad, 0, 1).reshape(1, rows, -1)
        return grad

    def own_block(mask):
        return lax.dynamic_index_in_dim(out_grad, me ^ mask, axis=1, keepdims=False)

    grads = []
    for mask in range(n_dp):
        block = own_block(mask)
        if mask:
            block = swap(block, "dp", n_dp, mask)
        grads.append(gather(block))

    far_gates = [swap(gate_pre[:, s : s + chunk], "dp", n_dp, far) for s in starts]
    near_gate = swap(gate_pre, "dp", n_dp, near)
    diag_gates = [swap(g, "dp", n_dp, near) for g in far_gates]

    input_part = jnp.dot(inputs, proj_in, preferred_element_type=jnp.float32)
    input_proj = sum_over(input_part, "tensor", n_tensor)

    far_query = swap(queries, "dp", n_dp, far)
    near_query = swap(queries, "dp", n_dp, near)
    diag_query = swap(far_query, "dp", n_dp, near)

    parts = [
        project(grads[0], gate_pre, down_weight, proj_out, 0, hidden, True),
        project(grads[1], near_gate, down_weight, proj_out, 0, hidden, True),
        0.0,
        0.0,
    ]
    for index, s in enumerate(starts):
        parts[2] += project(grads[2], far_gates[index], down_weight, proj_out, s, chunk, False)
        parts[3] += project(grads[3], diag_gates[index], down_weight, proj_out, s, chunk, False)

    grad_part = parts[0]
    for mask in range(1, n_dp):
        grad_part = grad_part + swap(parts[mask], "dp", n_dp, mask)
    grad_proj = sum_over(grad_part, "tensor", n_tensor)

    features = (
        (input_proj[:, :, None] * grad_proj[:, None, :]).reshape(rows, -1).astype(jnp.bfloat16)
    )
    width = queries.shape[1]
    all_queries = jnp.zeros((queries.shape[0], n_dp * width), queries.dtype)
    for mask, block in enumerate((queries, near_query, far_query, diag_query)):
        all_queries = lax.dynamic_update_slice(all_queries, block, (0, (me ^ mask) * width))
    return lax.dot_general(
        all_queries, features, (((1,), (1,)), ((), ())), preferred_element_type=jnp.float32
    )


def solution(mesh):
    return jax.shard_map(
        functools.partial(on_device, mesh.shape["dp"], mesh.shape["tensor"]),
        mesh=mesh,
        in_specs=(
            P(("parts", "dp"), "tensor"),
            P(("parts", "dp"), None, "tensor"),
            P(("parts", "dp"), "tensor"),
            P("tensor", "dp"),
            P("tensor", None),
            P("tensor", None),
            P("tensor", "dp"),
        ),
        out_specs=P("tensor", ("parts", "dp")),
        check_vma=False,
    )
```

```python
import functools

import jax
import jax.numpy as jnp
from jax import lax
from jax.experimental import pallas as pl
from jax.experimental.pallas import tpu as pltpu
from jax.sharding import PartitionSpec as P

LANES = 128
UNIT = 512
SUB = 256
VMEM = 60 * 1024 * 1024


def swap(value, axis, size, mask):
    return lax.ppermute(value, axis, [(i, i ^ mask) for i in range(size)])


def split_kernel(grad_ref, out_ref):
    me = lax.axis_index("dp")
    blocks = [grad_ref[:, k, :] for k in range(grad_ref.shape[1])]
    bit = 1
    while bit < len(blocks):
        flip = (me & bit) != 0
        blocks = [jnp.where(flip, blocks[k ^ bit], blocks[k]) for k in range(len(blocks))]
        bit *= 2
    for k, block in enumerate(blocks):
        out_ref[k] = block


def split_blocks(out_grad):
    rows, n, width = out_grad.shape
    step = rows // 4
    return pl.pallas_call(
        split_kernel,
        grid=(4,),
        in_specs=[pl.BlockSpec((step, n, width), lambda i: (i, 0, 0))],
        out_specs=pl.BlockSpec((n, step, width), lambda i: (0, i, 0)),
        out_shape=jax.ShapeDtypeStruct((n, rows, width), out_grad.dtype),
        compiler_params=pltpu.CompilerParams(vmem_limit_bytes=VMEM),
        name="split_blocks",
    )(out_grad)


def project_kernel(sub, grad_ref, gate_ref, own_ref, near_ref, proj_ref, *refs):
    out_ref, rows_ref, sems = refs[-3:]
    shards, pair, _, width = grad_ref.shape

    @pl.when(pl.program_id(0) == 0)
    def _():
        copies = [
            pltpu.make_async_copy(
                grad_ref.at[s, p], rows_ref.at[p, :, s * width : (s + 1) * width], sems.at[s, p]
            )
            for s in range(shards)
            for p in range(pair)
        ]
        for copy in copies:
            copy.start()
        out_ref[...] = jnp.zeros_like(out_ref)
        for copy in copies:
            copy.wait()

    total = out_ref[...]
    for start in range(0, gate_ref.shape[1], sub):
        hidden = None
        for p, weight_ref in enumerate((own_ref, near_ref)):
            term = lax.dot_general(
                rows_ref[p],
                weight_ref[start : start + sub, :],
                (((1,), (1,)), ((), ())),
                preferred_element_type=jnp.float32,
            )
            hidden = term if hidden is None else hidden + term
        gate = gate_ref[:, start : start + sub].astype(jnp.float32)
        below = 1.0 + jnp.exp(-gate)
        inverse = pl.reciprocal(below, approx=True)
        inverse = inverse * (2.0 - below * inverse)
        up_grad = (hidden * (gate * inverse)).astype(jnp.bfloat16)
        total += jnp.dot(
            up_grad, proj_ref[start : start + sub, :], preferred_element_type=jnp.float32
        )
    out_ref[...] = total


def project(grad, gate, weights, proj, offset, span, gate_row, gate_column, after):
    shards, pair, rows, width = grad.shape
    tile = UNIT if span % UNIT == 0 else span
    sub = SUB if tile % SUB == 0 else tile
    first = offset // tile
    gate_first = gate_column // tile
    gate_block = gate_row // rows
    depth = shards * width
    return pl.pallas_call(
        functools.partial(project_kernel, sub),
        grid=(span // tile,),
        in_specs=[
            pl.BlockSpec(memory_space=pl.ANY),
            pl.BlockSpec((rows, tile), lambda i: (gate_block, gate_first + i)),
            pl.BlockSpec((tile, depth), lambda i: (first + i, 0)),
            pl.BlockSpec((tile, depth), lambda i: (first + i, 0)),
            pl.BlockSpec((tile, proj.shape[1]), lambda i: (first + i, 0)),
        ]
        + [pl.BlockSpec(memory_space=pl.ANY)] * len(after),
        out_specs=pl.BlockSpec((rows, proj.shape[1]), lambda i: (0, 0)),
        out_shape=jax.ShapeDtypeStruct((rows, proj.shape[1]), jnp.float32),
        scratch_shapes=[
            pltpu.VMEM((pair, rows, depth), grad.dtype),
            pltpu.SemaphoreType.DMA((shards, pair)),
        ],
        compiler_params=pltpu.CompilerParams(vmem_limit_bytes=VMEM),
        cost_estimate=pl.CostEstimate(
            flops=2 * rows * span * (pair * depth + 4 * proj.shape[1]),
            bytes_accessed=2 * span * (pair * depth + rows),
            transcendentals=rows * span,
        ),
        name="project",
    )(grad, gate, *weights, proj, *after)


def sum_over(value, axis, size):
    mask = 1
    while mask < size:
        value = value + swap(value, axis, size, mask)
        mask *= 2
    return value


def chunks_of(hidden):
    units = hidden // UNIT
    if hidden % UNIT or units < 8:
        return [(0, hidden)]
    cuts = [0] + [max(1, round(units * part)) for part in (2 / 7, 4 / 7, 11 / 14)] + [units - 1, units]
    return [(a * UNIT, (b - a) * UNIT) for a, b in zip(cuts, cuts[1:]) if b > a]


def on_device(n_dp, n_tensor, inputs, out_grad, gate_pre, down_weight, proj_in, proj_out, queries):
    rows = out_grad.shape[0]
    half = rows // 2
    hidden = gate_pre.shape[1]
    me = lax.axis_index("dp")
    far, near = n_dp // 2, 1

    def gather(block):
        grad = lax.all_gather(block, "tensor", axis=0, tiled=False)
        if block.shape[2] % LANES:
            grad = jnp.transpose(grad, (1, 2, 0, 3)).reshape(1, 2, block.shape[1], -1)
        return grad

    chunks = chunks_of(hidden)
    far_gates = [swap(gate_pre[:, s : s + n], "dp", n_dp, far) for s, n in chunks]

    blocks = split_blocks(out_grad)
    far_blocks = swap(blocks[2:], "dp", n_dp, far)
    grads_a = gather(blocks[:2, :half])
    grads_far = gather(far_blocks)
    grads_b = gather(blocks[:2, half:])

    weights = (down_weight, swap(down_weight, "dp", n_dp, near))

    input_part = jnp.dot(inputs, proj_in, preferred_element_type=jnp.float32)
    input_proj = sum_over(input_part, "tensor", n_tensor)

    far_query = swap(queries, "dp", n_dp, far)
    near_query = swap(queries, "dp", n_dp, near)
    diag_query = swap(far_query, "dp", n_dp, near)

    width = queries.shape[1]
    all_queries = jnp.zeros((queries.shape[0], n_dp * width), queries.dtype)
    for mask, block in enumerate((queries, near_query, far_query, diag_query)):
        all_queries = lax.dynamic_update_slice(all_queries, block, (0, (me ^ mask) * width))

    own_a = project(grads_a, gate_pre, weights, proj_out, 0, hidden, 0, 0, (input_proj,))
    after = (own_a, all_queries)
    far_sum = None
    own_b = None
    for index, (s, n) in enumerate(chunks):
        if index == len(chunks) - 1:
            own_b = project(grads_b, gate_pre, weights, proj_out, 0, hidden, half, 0, after)
            after = (own_b,)
        part = project(grads_far, far_gates[index], weights, proj_out, s, n, 0, 0, after)
        far_sum = part if far_sum is None else far_sum + part
        after = (part,)

    grad_part = jnp.concatenate([own_a, own_b]) + swap(far_sum, "dp", n_dp, far)
    grad_proj = sum_over(grad_part, "tensor", n_tensor)

    features = (
        (input_proj[:, :, None] * grad_proj[:, None, :]).reshape(rows, -1).astype(jnp.bfloat16)
    )
    return lax.dot_general(
        all_queries, features, (((1,), (1,)), ((), ())), preferred_element_type=jnp.float32
    )


def solution(mesh):
    return jax.shard_map(
        functools.partial(on_device, mesh.shape["dp"], mesh.shape["tensor"]),
        mesh=mesh,
        in_specs=(
            P(("parts", "dp"), "tensor"),
            P(("parts", "dp"), None, "tensor"),
            P(("parts", "dp"), "tensor"),
            P("tensor", "dp"),
            P("tensor", None),
            P("tensor", None),
            P("tensor", "dp"),
        ),
        out_specs=P("tensor", ("parts", "dp")),
        check_vma=False,
    )
```

```python
import functools

import jax
import jax.numpy as jnp
from jax import lax
from jax.experimental import pallas as pl
from jax.experimental.pallas import tpu as pltpu
from jax.sharding import PartitionSpec as P

LANES = 128
TILE = 512
RING = 4
VMEM = 60 * 1024 * 1024
ANY = pl.BlockSpec(memory_space=pl.ANY)


def swap(value, axis, size, mask):
    return lax.ppermute(value, axis, [(i, i ^ mask) for i in range(size)])


def split_kernel(grad_ref, *refs):
    me = lax.axis_index("dp")
    own_ref, far_ref = refs[-2:]
    blocks = [grad_ref[:, k, :] for k in range(grad_ref.shape[1])]
    bit = 1
    while bit < len(blocks):
        flip = (me & bit) != 0
        blocks = [jnp.where(flip, blocks[k ^ bit], blocks[k]) for k in range(len(blocks))]
        bit *= 2
    half = len(blocks) // 2
    for k in range(half):
        own_ref[k] = blocks[k]
        far_ref[k] = blocks[half + k]


def split_blocks(out_grad, after):
    rows, n, width = out_grad.shape
    step = rows // 4
    out = jax.ShapeDtypeStruct((n // 2, rows, width), out_grad.dtype)
    return pl.pallas_call(
        split_kernel,
        grid=(4,),
        in_specs=[pl.BlockSpec((step, n, width), lambda i: (i, 0, 0))] + [ANY] * len(after),
        out_specs=[pl.BlockSpec((n // 2, step, width), lambda i: (0, i, 0))] * 2,
        out_shape=[out, out],
        compiler_params=pltpu.CompilerParams(vmem_limit_bytes=VMEM),
        name="split_blocks",
    )(out_grad, *after)


def project_kernel(tiles, pieces, chained, *refs):
    grads = refs[:pieces]
    gate_ref, own_ref, near_ref, proj_ref = refs[pieces : pieces + 4]
    before_ref = refs[pieces + 4] if chained else None
    out_ref, rows_ref, even_ref, odd_ref, sum_ref, sems = refs[-6:]
    step = pl.program_id(0)
    pair, _, width = grads[0].shape

    def fill():
        shard = lax.axis_index("tensor")
        copies = []
        for k, grad_ref in enumerate(grads):
            column = lax.rem(shard + pieces - k, pieces) * width if pieces > 1 else 0
            columns = pl.ds(pl.multiple_of(column, width), width) if pieces > 1 else slice(None)
            for p in range(pair):
                copies.append(
                    pltpu.make_async_copy(grad_ref.at[p], rows_ref.at[p, :, columns], sems.at[k, p])
                )
        for copy in copies:
            copy.start()
        sum_ref[...] = jnp.zeros_like(sum_ref)
        for copy in copies:
            copy.wait()

    def multiply(hidden_ref):
        hidden = None
        for p, weight_ref in enumerate((own_ref, near_ref)):
            term = lax.dot_general(
                rows_ref[p],
                weight_ref[...],
                (((1,), (1,)), ((), ())),
                preferred_element_type=jnp.float32,
            )
            hidden = term if hidden is None else hidden + term
        hidden_ref[...] = hidden

    def reduce(hidden_ref):
        gate = gate_ref[...].astype(jnp.float32)
        below = 1.0 + jnp.exp(-gate)
        inverse = pl.reciprocal(below, approx=True)
        inverse = inverse * (2.0 - below * inverse)
        up_grad = (hidden_ref[...] * (gate * inverse)).astype(jnp.bfloat16)
        sum_ref[...] += jnp.dot(up_grad, proj_ref[...], preferred_element_type=jnp.float32)

    @pl.when(step == 0)
    def _():
        fill()
        multiply(even_ref)

    @pl.when((step > 0) & (step < tiles) & (lax.rem(step, 2) == 1))
    def _():
        reduce(even_ref)
        multiply(odd_ref)

    @pl.when((step > 0) & (step < tiles) & (lax.rem(step, 2) == 0))
    def _():
        reduce(odd_ref)
        multiply(even_ref)

    @pl.when(step == tiles)
    def _():
        reduce(even_ref if tiles % 2 else odd_ref)
        total = sum_ref[...].T
        out_ref[...] = total + before_ref[...] if chained else total


def project(grads, gate, weights, proj, offset, span, gate_column, before, after):
    pieces = len(grads)
    pair, rows, width = grads[0].shape
    depth = weights[0].shape[1]
    k = proj.shape[1]
    tile = TILE if span % TILE == 0 else span
    tiles = span // tile
    first, gate_first = offset // tile, gate_column // tile
    now = lambda i: first + jnp.minimum(i, tiles - 1)
    last = lambda i: jnp.maximum(i - 1, 0)
    chained = before is not None
    total = pl.BlockSpec((k, rows), lambda i: (0, 0))
    return pl.pallas_call(
        functools.partial(project_kernel, tiles, pieces, chained),
        grid=(tiles + 1,),
        in_specs=[ANY] * pieces
        + [
            pl.BlockSpec((rows, tile), lambda i: (0, gate_first + last(i))),
            pl.BlockSpec((tile, depth), lambda i: (now(i), 0)),
            pl.BlockSpec((tile, depth), lambda i: (now(i), 0)),
            pl.BlockSpec((tile, k), lambda i: (first + last(i), 0)),
        ]
        + [total] * chained
        + [ANY] * len(after),
        out_specs=total,
        out_shape=jax.ShapeDtypeStruct((k, rows), jnp.float32),
        scratch_shapes=[
            pltpu.VMEM((pair, rows, depth), grads[0].dtype),
            pltpu.VMEM((rows, tile), jnp.float32),
            pltpu.VMEM((rows, tile), jnp.float32),
            pltpu.VMEM((rows, k), jnp.float32),
            pltpu.SemaphoreType.DMA((pieces, pair)),
        ],
        compiler_params=pltpu.CompilerParams(vmem_limit_bytes=VMEM),
        cost_estimate=pl.CostEstimate(
            flops=2 * rows * span * (pair * depth + 4 * k),
            bytes_accessed=2 * span * (pair * depth + rows),
            transcendentals=rows * span,
        ),
        name="project",
    )(*grads, gate, *weights, proj, *([before] if chained else []), *after)


def score_kernel(input_ref, grad_ref, other_ref, query_ref, out_ref):
    grad = grad_ref[...] + other_ref[...]
    high = grad.astype(jnp.bfloat16)
    low = (grad - high.astype(jnp.float32)).astype(jnp.bfloat16)
    both = jnp.concatenate([high, low], axis=0)
    total = jnp.zeros_like(out_ref)
    for i in range(query_ref.shape[0]):
        part = jnp.dot(query_ref[i], both, preferred_element_type=jnp.float32)
        total += input_ref[i : i + 1, :] * part
    out_ref[...] = total


def score(input_proj, grad, other, queries):
    k, rows = grad.shape
    count = queries.shape[0]
    pairs = queries.reshape(count, k, k).transpose(1, 0, 2)
    pairs = jnp.concatenate([pairs, pairs], axis=2)
    return pairs, lambda grad, other, pairs: pl.pallas_call(
        score_kernel,
        out_shape=jax.ShapeDtypeStruct((count, rows), jnp.float32),
        compiler_params=pltpu.CompilerParams(vmem_limit_bytes=VMEM),
        name="score",
    )(input_proj, grad, other, pairs)


def chunks_of(hidden):
    units = hidden // TILE
    if hidden % TILE or units < 8:
        return [(0, hidden)]
    cuts = [0, round(units / 7), units - 3, units - 1, units]
    return [(a * TILE, (b - a) * TILE) for a, b in zip(cuts, cuts[1:]) if b > a]


def on_device(n_dp, n_tensor, inputs, out_grad, gate_pre, down_weight, proj_in, proj_out, queries):
    rows = out_grad.shape[0]
    hidden = gate_pre.shape[1]
    me = lax.axis_index("dp")
    far, near = n_dp // 2, 1

    def gather(block, hold=None):
        if n_tensor > RING or block.shape[2] % LANES:
            grad = lax.all_gather(block, "tensor", axis=0, tiled=False)
            return [jnp.transpose(grad, (1, 2, 0, 3)).reshape(2, rows, -1)]
        pieces = [block]
        for k in range(n_tensor - 1):
            piece = pieces[-1]
            if k == 1 and hold is not None:
                piece, _ = lax.optimization_barrier((piece, hold))
                pieces[-1] = piece
            pieces.append(
                lax.ppermute(piece, "tensor", [(i, (i + 1) % n_tensor) for i in range(n_tensor)])
            )
        return pieces

    chunks = chunks_of(hidden)
    weights = (down_weight, swap(down_weight, "dp", n_dp, near))

    far_query = swap(queries, "dp", n_dp, far)
    near_query = swap(queries, "dp", n_dp, near)
    diag_query = swap(far_query, "dp", n_dp, near)

    def cut(source, chunk):
        return source[:, chunk[0] : chunk[0] + chunk[1]]

    first = cut(gate_pre, chunks[0])
    own_blocks, far_blocks = split_blocks(out_grad, (first,))
    later = [cut(gate_pre, chunk) for chunk in chunks[1:]]
    if later:
        later[0], far_blocks, _ = lax.optimization_barrier((later[0], far_blocks, far_query))
    far_gates = [swap(part, "dp", n_dp, far) for part in [first] + later]
    grads_own = gather(own_blocks, far_gates[0])
    grads_far = gather(swap(far_blocks, "dp", n_dp, far))

    input_proj = lax.dot_general(
        proj_in, inputs, (((0,), (1,)), ((), ())), preferred_element_type=jnp.float32
    )
    mask = 1
    while mask < n_tensor:
        input_proj = input_proj + swap(input_proj, "tensor", n_tensor, mask)
        mask *= 2

    width = queries.shape[1]
    all_queries = jnp.zeros((queries.shape[0], n_dp * width), queries.dtype)
    for mask, block in enumerate((queries, near_query, far_query, diag_query)):
        all_queries = lax.dynamic_update_slice(all_queries, block, (0, (me ^ mask) * width))
    pairs, finish = score(input_proj, input_proj, input_proj, all_queries)

    middle = hidden // 2 if hidden % (2 * TILE) == 0 else 0
    own_sum = None
    after = (input_proj, pairs)
    for s, n in ((0, middle), (middle, hidden - middle)):
        if n:
            own_sum = project(grads_own, gate_pre, weights, proj_out, s, n, s, own_sum, after)
            after = (own_sum,)
    far_sum = None
    for gate, (s, n) in zip(far_gates, chunks):
        far_sum = project(grads_far, gate, weights, proj_out, s, n, 0, far_sum, after)
        after = ()

    value = own_sum + swap(far_sum, "dp", n_dp, far)
    mask = 1
    while mask < n_tensor:
        other = swap(value, "tensor", n_tensor, mask)
        mask *= 2
        if mask < n_tensor:
            value = value + other
    return finish(value, other, pairs)


def solution(mesh):
    return jax.shard_map(
        functools.partial(on_device, mesh.shape["dp"], mesh.shape["tensor"]),
        mesh=mesh,
        in_specs=(
            P(("parts", "dp"), "tensor"),
            P(("parts", "dp"), None, "tensor"),
            P(("parts", "dp"), "tensor"),
            P("tensor", "dp"),
            P("tensor", None),
            P("tensor", None),
            P("tensor", "dp"),
        ),
        out_specs=P("tensor", ("parts", "dp")),
        check_vma=False,
    )
```

```python
import functools

import jax
import jax.numpy as jnp
from jax import lax
from jax.experimental import pallas as pl
from jax.experimental.pallas import tpu as pltpu
from jax.sharding import PartitionSpec as P

TILE = 512
RING = 4
VMEM = 60 * 1024 * 1024
ANY = pl.BlockSpec(memory_space=pl.ANY)


def swap(value, axis, size, mask):
    return lax.ppermute(value, axis, [(i, i ^ mask) for i in range(size)])


def split_kernel(grad_ref, *refs):
    me = lax.axis_index("dp")
    own_ref, far_ref = refs[-2:]
    blocks = [grad_ref[:, k, :] for k in range(grad_ref.shape[1])]
    bit = 1
    while bit < len(blocks):
        flip = (me & bit) != 0
        blocks = [jnp.where(flip, blocks[k ^ bit], blocks[k]) for k in range(len(blocks))]
        bit *= 2
    half = len(blocks) // 2
    for k in range(half):
        own_ref[k] = blocks[k].T
        far_ref[k] = blocks[half + k].T


def split_blocks(out_grad, after):
    rows, n, width = out_grad.shape
    step = rows // 4
    out = jax.ShapeDtypeStruct((n // 2, width, rows), out_grad.dtype)
    return pl.pallas_call(
        split_kernel,
        grid=(4,),
        in_specs=[pl.BlockSpec((step, n, width), lambda i: (i, 0, 0))] + [ANY] * len(after),
        out_specs=[pl.BlockSpec((n // 2, width, step), lambda i: (0, 0, i))] * 2,
        out_shape=[out, out],
        compiler_params=pltpu.CompilerParams(vmem_limit_bytes=VMEM),
        name="split_blocks",
    )(out_grad, *after)


def project_kernel(tiles, pieces, chained, *refs):
    grads = refs[:pieces]
    gate_ref, own_ref, near_ref, proj_ref = refs[pieces : pieces + 4]
    before_ref = refs[pieces + 4] if chained else None
    out_ref, rows_ref, even_ref, odd_ref, sum_ref, sems = refs[-6:]
    step = pl.program_id(0)
    pair, width, _ = grads[0].shape

    def fill():
        shard = lax.axis_index("tensor")
        copies = []
        for k, grad_ref in enumerate(grads):
            place = slice(None)
            if pieces > 1:
                place = pl.ds(pl.multiple_of(lax.rem(shard + pieces - k, pieces) * width, width), width)
            for p in range(pair):
                copies.append(
                    pltpu.make_async_copy(grad_ref.at[p], rows_ref.at[p, place], sems.at[k, p])
                )
        for copy in copies:
            copy.start()
        sum_ref[...] = jnp.zeros_like(sum_ref)
        for copy in copies:
            copy.wait()

    def multiply(hidden_ref):
        hidden_ref[...] = jnp.dot(
            own_ref[...], rows_ref[0], preferred_element_type=jnp.float32
        ) + jnp.dot(near_ref[...], rows_ref[1], preferred_element_type=jnp.float32)

    def reduce(hidden_ref):
        gate = gate_ref[...].T.astype(jnp.float32)
        silu = gate * (0.5 + 0.5 * jnp.tanh(0.5 * gate))
        up_grad = (hidden_ref[...] * silu).astype(jnp.bfloat16)
        sum_ref[...] += jnp.dot(proj_ref[...], up_grad, preferred_element_type=jnp.float32)

    @pl.when(step == 0)
    def _():
        fill()
        multiply(even_ref)

    @pl.when((step > 0) & (step < tiles) & (lax.rem(step, 2) == 1))
    def _():
        reduce(even_ref)
        multiply(odd_ref)

    @pl.when((step > 0) & (step < tiles) & (lax.rem(step, 2) == 0))
    def _():
        reduce(odd_ref)
        multiply(even_ref)

    @pl.when(step == tiles)
    def _():
        reduce(even_ref if tiles % 2 else odd_ref)
        total = sum_ref[...]
        out_ref[...] = total + before_ref[...] if chained else total


def project(grads, gate, weights, proj, offset, span, gate_column, before, after):
    pieces = len(grads)
    pair, _, rows = grads[0].shape
    depth = weights[0].shape[1]
    k = proj.shape[0]
    tile = TILE if span % TILE == 0 else span
    tiles = span // tile
    first, gate_first = offset // tile, gate_column // tile
    now = lambda i: first + jnp.minimum(i, tiles - 1)
    last = lambda i: jnp.maximum(i - 1, 0)
    chained = before is not None
    total = pl.BlockSpec((k, rows), lambda i: (0, 0))
    return pl.pallas_call(
        functools.partial(project_kernel, tiles, pieces, chained),
        grid=(tiles + 1,),
        in_specs=[ANY] * pieces
        + [
            pl.BlockSpec((rows, tile), lambda i: (0, gate_first + last(i))),
            pl.BlockSpec((tile, depth), lambda i: (now(i), 0)),
            pl.BlockSpec((tile, depth), lambda i: (now(i), 0)),
            pl.BlockSpec((k, tile), lambda i: (0, first + last(i))),
        ]
        + [total] * chained
        + [ANY] * len(after),
        out_specs=total,
        out_shape=jax.ShapeDtypeStruct((k, rows), jnp.float32),
        scratch_shapes=[
            pltpu.VMEM((pair, depth, rows), grads[0].dtype),
            pltpu.VMEM((tile, rows), jnp.float32),
            pltpu.VMEM((tile, rows), jnp.float32),
            pltpu.VMEM((k, rows), jnp.float32),
            pltpu.SemaphoreType.DMA((pieces, pair)),
        ],
        compiler_params=pltpu.CompilerParams(vmem_limit_bytes=VMEM),
        cost_estimate=pl.CostEstimate(
            flops=2 * rows * span * (pair * depth + 4 * k),
            bytes_accessed=2 * span * (pair * depth + rows),
            transcendentals=rows * span,
        ),
        name="project",
    )(*grads, gate, *weights, proj, *([before] if chained else []), *after)


def score_kernel(input_ref, grad_ref, other_ref, query_ref, out_ref):
    grad = grad_ref[...] + other_ref[...]
    high = grad.astype(jnp.bfloat16)
    low = (grad - high.astype(jnp.float32)).astype(jnp.bfloat16)
    both = jnp.concatenate([high, low], axis=0)
    total = jnp.zeros_like(out_ref)
    for i in range(query_ref.shape[0]):
        part = jnp.dot(query_ref[i], both, preferred_element_type=jnp.float32)
        total += input_ref[i : i + 1, :] * part
    out_ref[...] = total


def pair_queries(queries, k):
    pairs = queries.reshape(queries.shape[0], k, k).transpose(1, 0, 2)
    return jnp.concatenate([pairs, pairs], axis=2)


def score(input_proj, grad, other, pairs):
    return pl.pallas_call(
        score_kernel,
        out_shape=jax.ShapeDtypeStruct((pairs.shape[1], grad.shape[1]), jnp.float32),
        compiler_params=pltpu.CompilerParams(vmem_limit_bytes=VMEM),
        name="score",
    )(input_proj, grad, other, pairs)


def chunks_of(hidden):
    units = hidden // TILE
    if hidden % TILE or units < 8:
        return [(0, hidden)]
    cuts = [0, round(units / 7), units - 3, units - 1, units]
    return [(a * TILE, (b - a) * TILE) for a, b in zip(cuts, cuts[1:]) if b > a]


def on_device(n_dp, n_tensor, inputs, out_grad, gate_pre, down_weight, proj_in, proj_out, queries):
    rows = out_grad.shape[0]
    hidden = gate_pre.shape[1]
    me = lax.axis_index("dp")
    far, near = n_dp // 2, 1

    def gather(block, holds):
        if n_tensor > RING:
            grad = lax.all_gather(block, "tensor", axis=0, tiled=False)
            return [jnp.transpose(grad, (1, 0, 2, 3)).reshape(2, -1, rows)]
        pieces = [block]
        for k in range(n_tensor - 1):
            piece = pieces[-1]
            if k in holds:
                piece, _ = lax.optimization_barrier((piece, holds[k]))
                pieces[-1] = piece
            pieces.append(
                lax.ppermute(piece, "tensor", [(i, (i + 1) % n_tensor) for i in range(n_tensor)])
            )
        return pieces

    chunks = chunks_of(hidden)
    weights = (down_weight, swap(down_weight, "dp", n_dp, near))

    far_query = swap(queries, "dp", n_dp, far)
    near_query = swap(queries, "dp", n_dp, near)
    diag_query = swap(far_query, "dp", n_dp, near)

    def cut(source, chunk):
        return source[:, chunk[0] : chunk[0] + chunk[1]]

    first = cut(gate_pre, chunks[0])
    own_blocks, far_blocks = split_blocks(out_grad, (first,))
    later = [cut(gate_pre, chunk) for chunk in chunks[1:]]
    if later:
        later[0], far_blocks, _ = lax.optimization_barrier((later[0], far_blocks, far_query))
    far_gates = [swap(part, "dp", n_dp, far) for part in [first] + later]
    grads_own = gather(own_blocks, {1: far_gates[0]})

    input_proj = lax.dot_general(
        proj_in, inputs, (((0,), (1,)), ((), ())), preferred_element_type=jnp.float32
    )
    width = queries.shape[1]
    all_queries = jnp.zeros((queries.shape[0], n_dp * width), queries.dtype)
    for mask, block in enumerate((queries, near_query, far_query, diag_query)):
        all_queries = lax.dynamic_update_slice(all_queries, block, (0, (me ^ mask) * width))
    pairs = pair_queries(all_queries, proj_in.shape[1])

    middle = hidden // 2 if hidden % (2 * TILE) == 0 else 0
    own_sum = None
    after = (pairs,)
    proj_out = proj_out.T
    for s, n in ((0, middle), (middle, hidden - middle)):
        if n:
            own_sum = project(grads_own, gate_pre, weights, proj_out, s, n, s, own_sum, after)
            if after[0] is pairs:
                grads_far = gather(swap(far_blocks, "dp", n_dp, far), {2: own_sum})
            after = (own_sum,)
    input_proj, own_sum = lax.optimization_barrier((input_proj, own_sum))
    mask = 1
    while mask < n_tensor:
        input_proj = input_proj + swap(input_proj, "tensor", n_tensor, mask)
        mask *= 2
    far_sum = None
    for gate, (s, n) in zip(far_gates, chunks):
        if s + n == hidden:
            after += (input_proj,)
        far_sum = project(grads_far, gate, weights, proj_out, s, n, 0, far_sum, after)
        after = ()

    value = own_sum + swap(far_sum, "dp", n_dp, far)
    mask = 1
    while mask < n_tensor:
        other = swap(value, "tensor", n_tensor, mask)
        mask *= 2
        if mask < n_tensor:
            value = value + other
    return score(input_proj, value, other, pairs)


def solution(mesh):
    return jax.shard_map(
        functools.partial(on_device, mesh.shape["dp"], mesh.shape["tensor"]),
        mesh=mesh,
        in_specs=(
            P(("parts", "dp"), "tensor"),
            P(("parts", "dp"), None, "tensor"),
            P(("parts", "dp"), "tensor"),
            P("tensor", "dp"),
            P("tensor", None),
            P("tensor", None),
            P("tensor", "dp"),
        ),
        out_specs=P("tensor", ("parts", "dp")),
        check_vma=False,
    )
```

```python
import functools

import jax
import jax.numpy as jnp
from jax import lax
from jax.experimental import pallas as pl
from jax.experimental.pallas import tpu as pltpu
from jax.sharding import PartitionSpec as P

TILE = 512
RING = 4
VMEM = 60 * 1024 * 1024
ANY = pl.BlockSpec(memory_space=pl.ANY)


def swap(value, axis, size, mask):
    return lax.ppermute(value, axis, [(i, i ^ mask) for i in range(size)])


def split_kernel(first, grad_ref, *refs):
    me = lax.axis_index("dp")
    out_ref = refs[-1]
    blocks = [grad_ref[:, k, :] for k in range(grad_ref.shape[1])]
    bit = 1
    while bit < len(blocks):
        flip = (me & bit) != 0
        blocks = [jnp.where(flip, blocks[k ^ bit], blocks[k]) for k in range(len(blocks))]
        bit *= 2
    for k in range(out_ref.shape[0]):
        out_ref[k] = blocks[first + k].T


def split_blocks(out_grad, first, after):
    rows, n, width = out_grad.shape
    step = rows // 4
    return pl.pallas_call(
        functools.partial(split_kernel, first),
        grid=(4,),
        in_specs=[pl.BlockSpec((step, n, width), lambda i: (i, 0, 0))] + [ANY] * len(after),
        out_specs=pl.BlockSpec((n // 2, width, step), lambda i: (0, 0, i)),
        out_shape=jax.ShapeDtypeStruct((n // 2, width, rows), out_grad.dtype),
        compiler_params=pltpu.CompilerParams(vmem_limit_bytes=VMEM),
        name="split_blocks",
    )(out_grad, *after)


def gated(hidden, gate_ref, proj_ref):
    gate = gate_ref[...].T.astype(jnp.float32)
    silu = gate * (0.5 + 0.5 * jnp.tanh(0.5 * gate))
    up_grad = (hidden * silu).astype(jnp.bfloat16)
    return jnp.dot(proj_ref[...], up_grad, preferred_element_type=jnp.float32)


def project_kernel(tiles, ahead, pieces, chained, *refs):
    grads = refs[:pieces]
    gate_ref, own_ref, near_ref, proj_ref = refs[pieces : pieces + 4]
    before_ref = refs[pieces + 4] if chained else None
    later_ref = refs[-6] if ahead else None
    out_ref = refs[-7] if ahead else refs[-6]
    rows_ref, even_ref, odd_ref, sum_ref, sems = refs[-5:]
    step = pl.program_id(0)
    pair, width, _ = grads[0].shape

    def fill():
        shard = lax.axis_index("tensor")
        copies = []
        for k, grad_ref in enumerate(grads):
            place = slice(None)
            if pieces > 1:
                place = pl.ds(pl.multiple_of(lax.rem(shard + pieces - k, pieces) * width, width), width)
            for p in range(pair):
                copies.append(
                    pltpu.make_async_copy(grad_ref.at[p], rows_ref.at[p, place], sems.at[k, p])
                )
        for copy in copies:
            copy.start()
        sum_ref[...] = jnp.zeros_like(sum_ref)
        for copy in copies:
            copy.wait()

    def multiply(hidden_ref):
        hidden_ref[...] = jnp.dot(
            own_ref[...], rows_ref[0], preferred_element_type=jnp.float32
        ) + jnp.dot(near_ref[...], rows_ref[1], preferred_element_type=jnp.float32)

    def reduce(hidden_ref):
        sum_ref[...] += gated(hidden_ref[...], gate_ref, proj_ref)

    @pl.when(step == 0)
    def _():
        fill()
        multiply(even_ref)

    @pl.when((step > 0) & (step < tiles) & (lax.rem(step, 2) == 1))
    def _():
        reduce(even_ref)
        multiply(odd_ref)

    @pl.when((step > 0) & (step < tiles) & (lax.rem(step, 2) == 0))
    def _():
        reduce(odd_ref)
        multiply(even_ref)

    @pl.when(step == tiles)
    def _():
        reduce(even_ref if tiles % 2 else odd_ref)
        total = sum_ref[...]
        out_ref[...] = total + before_ref[...] if chained else total
        if ahead:
            multiply(later_ref)

    if ahead > 1:

        @pl.when(step > tiles)
        def _():
            multiply(later_ref)


def project(grads, gate, weights, proj, offset, span, extra, gate_column, before, after):
    pieces = len(grads)
    pair, _, rows = grads[0].shape
    depth = weights[0].shape[1]
    k = proj.shape[0]
    tile = TILE if span % TILE == 0 else span
    tiles = span // tile
    ahead = extra // tile
    first, gate_first = offset // tile, gate_column // tile
    now = lambda i: first + jnp.minimum(i, tiles + ahead - 1)
    last = lambda i: jnp.clip(i - 1, 0, tiles - 1)
    chained = before is not None
    total = pl.BlockSpec((k, rows), lambda i: (0, 0))
    later = pl.BlockSpec((tile, rows), lambda i: (jnp.maximum(i - tiles, 0), 0))
    return pl.pallas_call(
        functools.partial(project_kernel, tiles, ahead, pieces, chained),
        grid=(tiles + max(ahead, 1),),
        in_specs=[ANY] * pieces
        + [
            pl.BlockSpec((rows, tile), lambda i: (0, gate_first + last(i))),
            pl.BlockSpec((tile, depth), lambda i: (now(i), 0)),
            pl.BlockSpec((tile, depth), lambda i: (now(i), 0)),
            pl.BlockSpec((k, tile), lambda i: (0, first + last(i))),
        ]
        + [total] * chained
        + [ANY] * len(after),
        out_specs=[total] + [later] * bool(ahead),
        out_shape=[jax.ShapeDtypeStruct((k, rows), jnp.float32)]
        + [jax.ShapeDtypeStruct((extra, rows), jnp.float32)] * bool(ahead),
        scratch_shapes=[
            pltpu.VMEM((pair, depth, rows), grads[0].dtype),
            pltpu.VMEM((tile, rows), jnp.float32),
            pltpu.VMEM((tile, rows), jnp.float32),
            pltpu.VMEM((k, rows), jnp.float32),
            pltpu.SemaphoreType.DMA((pieces, pair)),
        ],
        compiler_params=pltpu.CompilerParams(vmem_limit_bytes=VMEM),
        cost_estimate=pl.CostEstimate(
            flops=2 * rows * (span + extra) * (pair * depth + 4 * k),
            bytes_accessed=2 * (span + extra) * (pair * depth + rows),
            transcendentals=rows * span,
        ),
        name="project",
    )(*grads, gate, *weights, proj, *([before] if chained else []), *after)


def finish_kernel(hidden_ref, gate_ref, proj_ref, before_ref, *refs):
    out_ref = refs[-1]

    @pl.when(pl.program_id(0) == 0)
    def _():
        out_ref[...] = before_ref[...]

    out_ref[...] += gated(hidden_ref[...], gate_ref, proj_ref)


def finish(hidden, gate, proj, offset, before, after):
    span, rows = hidden.shape
    k = proj.shape[0]
    first = offset // TILE
    total = pl.BlockSpec((k, rows), lambda i: (0, 0))
    return pl.pallas_call(
        finish_kernel,
        grid=(span // TILE,),
        in_specs=[
            pl.BlockSpec((TILE, rows), lambda i: (i, 0)),
            pl.BlockSpec((rows, TILE), lambda i: (0, i)),
            pl.BlockSpec((k, TILE), lambda i: (0, first + i)),
            total,
        ]
        + [ANY] * len(after),
        out_specs=total,
        out_shape=jax.ShapeDtypeStruct((k, rows), jnp.float32),
        compiler_params=pltpu.CompilerParams(vmem_limit_bytes=VMEM),
        name="finish",
    )(hidden, gate, proj, before, *after)


def score_kernel(input_ref, grad_ref, other_ref, query_ref, out_ref):
    grad = grad_ref[...] + other_ref[...]
    high = grad.astype(jnp.bfloat16)
    low = (grad - high.astype(jnp.float32)).astype(jnp.bfloat16)
    both = jnp.concatenate([high, low], axis=0)
    total = jnp.zeros_like(out_ref)
    for i in range(query_ref.shape[0]):
        part = jnp.dot(query_ref[i], both, preferred_element_type=jnp.float32)
        total += input_ref[i : i + 1, :] * part
    out_ref[...] = total


def pair_queries(queries, k):
    pairs = queries.reshape(queries.shape[0], k, k).transpose(1, 0, 2)
    return jnp.concatenate([pairs, pairs], axis=2)


def score(input_proj, grad, other, pairs):
    return pl.pallas_call(
        score_kernel,
        out_shape=jax.ShapeDtypeStruct((pairs.shape[1], grad.shape[1]), jnp.float32),
        compiler_params=pltpu.CompilerParams(vmem_limit_bytes=VMEM),
        name="score",
    )(input_proj, grad, other, pairs)


def chunks_of(hidden):
    units = hidden // TILE
    last = 3 * TILE if hidden % TILE == 0 and units >= 8 else 0
    return hidden - last, last


def on_device(n_dp, n_tensor, inputs, out_grad, gate_pre, down_weight, proj_in, proj_out, queries):
    rows = out_grad.shape[0]
    hidden = gate_pre.shape[1]
    me = lax.axis_index("dp")
    far, near = n_dp // 2, 1

    def gather(block, holds):
        if n_tensor > RING:
            grad = lax.all_gather(block, "tensor", axis=0, tiled=False)
            return [jnp.transpose(grad, (1, 0, 2, 3)).reshape(2, -1, rows)]
        pieces = [block]
        for k in range(n_tensor - 1):
            piece = pieces[-1]
            if k in holds:
                piece, _ = lax.optimization_barrier((piece, holds[k]))
                pieces[-1] = piece
            pieces.append(
                lax.ppermute(piece, "tensor", [(i, (i + 1) % n_tensor) for i in range(n_tensor)])
            )
        return pieces

    main, extra = chunks_of(hidden)
    weights = (down_weight, swap(down_weight, "dp", n_dp, near))

    far_query = swap(queries, "dp", n_dp, far)
    near_query = swap(queries, "dp", n_dp, near)
    diag_query = swap(far_query, "dp", n_dp, near)

    far_blocks = split_blocks(out_grad, n_dp // 2, ())
    own_blocks = split_blocks(out_grad, 0, (far_blocks,))
    far_blocks, _ = lax.optimization_barrier((far_blocks, far_query))
    far_start = swap(far_blocks, "dp", n_dp, far)
    gates, far_start = lax.optimization_barrier(
        ((gate_pre[:, :main], gate_pre[:, main:]), far_start)
    )
    far_gate, last_gate = (swap(part, "dp", n_dp, far) if part.size else None for part in gates)
    grads_own = gather(own_blocks, {})

    input_proj = lax.dot_general(
        proj_in, inputs, (((0,), (1,)), ((), ())), preferred_element_type=jnp.float32
    )
    width = queries.shape[1]
    all_queries = jnp.zeros((queries.shape[0], n_dp * width), queries.dtype)
    for mask, block in enumerate((queries, near_query, far_query, diag_query)):
        all_queries = lax.dynamic_update_slice(all_queries, block, (0, (me ^ mask) * width))
    pairs = pair_queries(all_queries, proj_in.shape[1])

    middle = hidden // 2 if hidden % (2 * TILE) == 0 else hidden
    proj_out = proj_out.T
    own_sum = None
    after = ()
    for s in range(0, hidden, middle):
        (own_sum,) = project(
            grads_own, gate_pre, weights, proj_out, s, middle, 0, s, own_sum, after
        )
        if s == 0:
            grads_far = gather(far_start, {2: own_sum})
        after = (own_sum,)
    input_proj, own_sum = lax.optimization_barrier((input_proj, own_sum))
    mask = 1
    while mask < n_tensor:
        input_proj = input_proj + swap(input_proj, "tensor", n_tensor, mask)
        mask *= 2
    far_sum, *later = project(
        grads_far, far_gate, weights, proj_out, 0, main, extra, 0, None, (own_sum,)
    )
    if extra:
        far_sum = finish(later[0], last_gate, proj_out, main, far_sum, (pairs, input_proj))

    value = own_sum + swap(far_sum, "dp", n_dp, far)
    mask = 1
    while mask < n_tensor:
        other = swap(value, "tensor", n_tensor, mask)
        mask *= 2
        if mask < n_tensor:
            value = value + other
    return score(input_proj, value, other, pairs)


def solution(mesh):
    return jax.shard_map(
        functools.partial(on_device, mesh.shape["dp"], mesh.shape["tensor"]),
        mesh=mesh,
        in_specs=(
            P(("parts", "dp"), "tensor"),
            P(("parts", "dp"), None, "tensor"),
            P(("parts", "dp"), "tensor"),
            P("tensor", "dp"),
            P("tensor", None),
            P("tensor", None),
            P("tensor", "dp"),
        ),
        out_specs=P("tensor", ("parts", "dp")),
        check_vma=False,
    )
```

```python
import functools

import jax
import jax.numpy as jnp
from jax import lax
from jax.experimental import pallas as pl
from jax.experimental.pallas import tpu as pltpu
from jax.sharding import PartitionSpec as P

TILE = 512
RING = 4
VMEM = 60 * 1024 * 1024
ANY = pl.BlockSpec(memory_space=pl.ANY)


def swap(value, axis, size, mask):
    return lax.ppermute(value, axis, [(i, i ^ mask) for i in range(size)])


def split_kernel(first, grad_ref, *refs):
    me = lax.axis_index("dp")
    out_ref = refs[-1]
    blocks = [grad_ref[:, k, :] for k in range(grad_ref.shape[1])]
    bit = 1
    while bit < len(blocks):
        flip = (me & bit) != 0
        blocks = [jnp.where(flip, blocks[k ^ bit], blocks[k]) for k in range(len(blocks))]
        bit *= 2
    for k in range(out_ref.shape[0]):
        out_ref[k] = blocks[first + k].T


def split_blocks(out_grad, first, after):
    rows, n, width = out_grad.shape
    step = rows // 4
    return pl.pallas_call(
        functools.partial(split_kernel, first),
        grid=(4,),
        in_specs=[pl.BlockSpec((step, n, width), lambda i: (i, 0, 0))] + [ANY] * len(after),
        out_specs=pl.BlockSpec((n // 2, width, step), lambda i: (0, 0, i)),
        out_shape=jax.ShapeDtypeStruct((n // 2, width, rows), out_grad.dtype),
        compiler_params=pltpu.CompilerParams(vmem_limit_bytes=VMEM),
        name="split_blocks",
    )(out_grad, *after)


def gated(hidden, gate_ref, proj_ref):
    gate = gate_ref[...].T.astype(jnp.float32)
    silu = gate * (0.5 + 0.5 * jnp.tanh(0.5 * gate))
    up_grad = (hidden * silu).astype(jnp.bfloat16)
    return jnp.dot(proj_ref[...], up_grad, preferred_element_type=jnp.float32)


def project_kernel(tiles, ahead, pieces, chained, carried, shard_ref, *refs):
    refs = list(refs)
    take = lambda n: [refs.pop(0) for _ in range(n)]
    grads = take(pieces)
    weights = take(2 * pieces)
    gate_ref, proj_ref = take(2) if tiles else (None, None)
    (before_ref,) = take(1) if chained else (None,)
    (partial_ref,) = take(1) if carried else (None,)
    sum_ref, odd_ref, even_ref = [refs.pop() for _ in range(3)] if tiles else (None,) * 3
    later_ref = refs.pop() if ahead else None
    out_ref = refs.pop() if tiles else None
    step = pl.program_id(0)

    def multiply(hidden_ref):
        hidden = partial_ref[...] if carried else None
        for k, grad_ref in enumerate(grads):
            for p in range(2):
                term = jnp.dot(
                    weights[2 * k + p][...], grad_ref[p], preferred_element_type=jnp.float32
                )
                hidden = term if hidden is None else hidden + term
        hidden_ref[...] = hidden

    if not tiles:
        multiply(later_ref)
        return

    def reduce(hidden_ref):
        sum_ref[...] += gated(hidden_ref[...], gate_ref, proj_ref)

    @pl.when(step == 0)
    def _():
        sum_ref[...] = before_ref[...] if chained else jnp.zeros_like(sum_ref)
        multiply(even_ref)

    @pl.when((step > 0) & (step < tiles) & (lax.rem(step, 2) == 1))
    def _():
        reduce(even_ref)
        multiply(odd_ref)

    @pl.when((step > 0) & (step < tiles) & (lax.rem(step, 2) == 0))
    def _():
        reduce(odd_ref)
        multiply(even_ref)

    @pl.when(step == tiles)
    def _():
        reduce(even_ref if tiles % 2 else odd_ref)
        out_ref[...] = sum_ref[...]
        if ahead:
            multiply(later_ref)

    if ahead > 1:

        @pl.when(step > tiles)
        def _():
            multiply(later_ref)


def project(shard, grads, gate, weights, proj, offset, span, extra, gate_column, before, partial, after):
    places = [place for place, _ in grads]
    pieces = [piece for _, piece in grads]
    _, width, rows = pieces[0].shape
    count = weights[0].shape[1] // width
    k = proj.shape[0]
    tile = TILE if (span + extra) % TILE == 0 else span + extra
    tiles, ahead = span // tile, extra // tile
    first, gate_first = offset // tile, gate_column // tile
    now = lambda i: jnp.minimum(i, tiles + ahead - 1)
    last = lambda i: jnp.clip(i - 1, 0, max(tiles - 1, 0))
    chained, carried = before is not None, partial is not None
    total = pl.BlockSpec((k, rows), lambda i, s: (0, 0))
    later = pl.BlockSpec((tile, rows), lambda i, s: (jnp.maximum(i - tiles, 0), 0))

    def weight_spec(place):
        return pl.BlockSpec(
            (tile, width), lambda i, s: (first + now(i), lax.rem(s[0] + count - place, count))
        )

    specs = [pl.BlockSpec((2, width, rows), lambda i, s: (0, 0, 0)) for _ in pieces]
    specs += [weight_spec(place) for place in places for _ in range(2)]
    operands = pieces + [weight for _ in places for weight in weights]
    if tiles:
        specs += [
            pl.BlockSpec((rows, tile), lambda i, s: (0, gate_first + last(i))),
            pl.BlockSpec((k, tile), lambda i, s: (0, first + last(i))),
        ]
        operands += [gate, proj]
    if chained:
        specs.append(total)
        operands.append(before)
    if carried:
        specs.append(pl.BlockSpec((tile, rows), lambda i, s: (first + now(i), 0)))
        operands.append(partial)
    hidden = pltpu.VMEM((tile, rows), jnp.float32)
    depth = 2 * width * len(pieces)
    return pl.pallas_call(
        functools.partial(project_kernel, tiles, ahead, len(pieces), chained, carried),
        grid_spec=pltpu.PrefetchScalarGridSpec(
            num_scalar_prefetch=1,
            grid=(tiles + max(ahead, 1) if tiles else ahead,),
            in_specs=specs + [ANY] * len(after),
            out_specs=[total] * bool(tiles) + [later] * bool(ahead),
            scratch_shapes=[hidden, hidden, pltpu.VMEM((k, rows), jnp.float32)] if tiles else [],
        ),
        out_shape=[jax.ShapeDtypeStruct((k, rows), jnp.float32)] * bool(tiles)
        + [jax.ShapeDtypeStruct((extra, rows), jnp.float32)] * bool(ahead),
        compiler_params=pltpu.CompilerParams(vmem_limit_bytes=VMEM),
        cost_estimate=pl.CostEstimate(
            flops=2 * rows * (span + extra) * depth,
            bytes_accessed=2 * (span + extra) * (depth + rows),
            transcendentals=rows * span,
        ),
        name="project",
    )(shard, *operands, *after)


def finish_kernel(hidden_ref, gate_ref, proj_ref, before_ref, *refs):
    out_ref, sum_ref = refs[-2:]
    part = gated(hidden_ref[...], gate_ref, proj_ref)

    @pl.when(pl.program_id(0) == 0)
    def _():
        sum_ref[...] = before_ref[...] + part

    @pl.when(pl.program_id(0) > 0)
    def _():
        sum_ref[...] += part

    @pl.when(pl.program_id(0) == pl.num_programs(0) - 1)
    def _():
        out_ref[...] = sum_ref[...].astype(out_ref.dtype)


def finish(hidden, gate, proj, offset, before, dtype, after):
    span, rows = hidden.shape
    k = proj.shape[0]
    first = offset // TILE
    total = pl.BlockSpec((k, rows), lambda i: (0, 0))
    return pl.pallas_call(
        finish_kernel,
        grid=(span // TILE,),
        in_specs=[
            pl.BlockSpec((TILE, rows), lambda i: (i, 0)),
            pl.BlockSpec((rows, TILE), lambda i: (0, i)),
            pl.BlockSpec((k, TILE), lambda i: (0, first + i)),
            total,
        ]
        + [ANY] * len(after),
        out_specs=total,
        out_shape=jax.ShapeDtypeStruct((k, rows), dtype),
        scratch_shapes=[pltpu.VMEM((k, rows), jnp.float32)],
        compiler_params=pltpu.CompilerParams(vmem_limit_bytes=VMEM),
        name="finish",
    )(hidden, gate, proj, before, *after)


def score_kernel(n_both, parts, out_ref):
    *parts, query_ref = parts
    total = lambda refs: functools.reduce(jnp.add, [ref[...].astype(jnp.float32) for ref in refs])
    grad = total(parts[n_both:])
    inputs, own = jnp.split(total(parts[:n_both]), 2)
    grad += own
    high = grad.astype(jnp.bfloat16)
    low = (grad - high.astype(jnp.float32)).astype(jnp.bfloat16)
    both = jnp.concatenate([high, low], axis=0)
    count = out_ref.shape[0]
    k = inputs.shape[0]
    group = 8
    scores = jnp.zeros(out_ref.shape, jnp.float32)
    for i in range(0, k, group):
        part = jnp.dot(
            query_ref[i * count : (i + group) * count, :], both, preferred_element_type=jnp.float32
        )
        for n in range(group):
            scores += inputs[i + n : i + n + 1, :] * part[n * count : (n + 1) * count, :]
    out_ref[...] = scores


def pair_queries(queries, k):
    pairs = queries.reshape(queries.shape[0], k, k).transpose(1, 0, 2).reshape(-1, k)
    return jnp.concatenate([pairs, pairs], axis=1)


def score(both, grads, pairs):
    k, rows = grads[0].shape
    return pl.pallas_call(
        lambda *refs: score_kernel(len(both), refs[:-1], refs[-1]),
        out_shape=jax.ShapeDtypeStruct((pairs.shape[0] // k, rows), jnp.float32),
        compiler_params=pltpu.CompilerParams(vmem_limit_bytes=VMEM),
        name="score",
    )(*both, *grads, pairs)


def chunks_of(hidden):
    units = hidden // TILE
    last = 3 * TILE if hidden % TILE == 0 and units >= 8 else 0
    return hidden - last, last


def on_device(n_dp, n_tensor, inputs, out_grad, gate_pre, down_weight, proj_in, proj_out, queries):
    rows = out_grad.shape[0]
    hidden = gate_pre.shape[1]
    me = lax.axis_index("dp")
    shard = lax.axis_index("tensor").astype(jnp.int32).reshape(1)
    far, near = n_dp // 2, 1
    ring = n_tensor <= RING
    main, extra = chunks_of(hidden)

    def onward(piece, hold=None):
        if hold is not None:
            piece, _ = lax.optimization_barrier((piece, hold))
        return lax.ppermute(piece, "tensor", [(i, (i + 1) % n_tensor) for i in range(n_tensor)])

    def gather(block):
        grad = lax.all_gather(block, "tensor", axis=0, tiled=False)
        return jnp.transpose(grad, (1, 0, 2, 3)).reshape(2, -1, rows)

    def spread(value, mask):
        if not ring:
            total = lax.psum(value.astype(jnp.float32), "tensor")
            return [swap(total, "dp", n_dp, mask) if mask else total]
        got = [value] if not mask else []
        for step in range(0 if mask else 1, n_tensor):
            pairs = [
                (z * n_dp + d, (z + step) % n_tensor * n_dp + (d ^ mask))
                for z in range(n_tensor)
                for d in range(n_dp)
            ]
            got.append(lax.ppermute(value, ("tensor", "dp"), pairs))
        return got

    weights = (down_weight, swap(down_weight, "dp", n_dp, near))
    far_query = swap(queries, "dp", n_dp, far)

    own_blocks = split_blocks(out_grad, 0, ())
    far_blocks = split_blocks(out_grad, n_dp // 2, (own_blocks,))
    far_blocks, _ = lax.optimization_barrier((far_blocks, far_query))
    far_start = swap(far_blocks, "dp", n_dp, far)
    own = [own_blocks, onward(own_blocks)] if ring and n_tensor > 1 else [own_blocks]
    gates, far_start, own[-1] = lax.optimization_barrier(
        ((gate_pre[:, :main], gate_pre[:, main:]), far_start, own[-1])
    )
    far_gate, last_gate = (swap(part, "dp", n_dp, far) if part.size else None for part in gates)

    def all_pairs(hold):
        blocks, _ = lax.optimization_barrier(((queries, far_query), hold))
        blocks += tuple(swap(block, "dp", n_dp, near) for block in blocks)
        width = queries.shape[1]
        merged = jnp.zeros((queries.shape[0], n_dp * width), queries.dtype)
        for mask, block in zip((0, far, near, far ^ near), blocks):
            merged = lax.dynamic_update_slice(merged, block, (0, (me ^ mask) * width))
        return pair_queries(merged, proj_in.shape[1])

    proj_out = proj_out.T
    if ring and n_tensor > 1:
        split = n_tensor // 2
        while len(own) <= split:
            own.append(onward(own[-1]))
        own_early = list(enumerate(own))[:split]
        (own_sum,) = project(
            shard, own_early, gate_pre, weights, proj_out, 0, hidden, 0, 0, None, None, ()
        )
        early_sum = own_sum
        pairs = all_pairs(early_sum)
        others = [far_start]
        for _ in range(split - 1):
            others.append(onward(others[-1]))
        far_early = list(enumerate(others))
        (partial,) = project(
            shard, far_early, None, weights, proj_out, 0, 0, hidden, 0, None, None, (own_sum,)
        )
        while len(own) < n_tensor:
            own.append(onward(own[-1], early_sum))
        own_late = list(enumerate(own))[split:]
        middle = hidden // 2 if hidden % (2 * TILE) == 0 else hidden
        after = (partial,)
        for s in range(0, hidden, middle):
            (own_sum,) = project(
                shard, own_late, gate_pre, weights, proj_out, s, middle, 0, s, own_sum, None, after
            )
            if s == 0:
                while len(others) < n_tensor:
                    hold = own_sum if len(others) == n_tensor - 1 else early_sum
                    others.append(onward(others[-1], hold))
            after = (pairs,)
        far_late = list(enumerate(others))[split:]
    else:
        (own_sum,) = project(
            shard, [(0, gather(own_blocks))], gate_pre, weights, proj_out, 0, hidden, 0, 0, None, None, ()
        )
        far_late, partial = [(0, gather(far_start))], None
        pairs = all_pairs(own_sum)

    input_part = lax.dot_general(
        proj_in, inputs, (((0,), (1,)), ((), ())), preferred_element_type=jnp.float32
    )
    both = jnp.concatenate([input_part, own_sum])
    places = [place for place, _ in far_late]
    both, far_gate, pieces = lax.optimization_barrier((both, far_gate, [p for _, p in far_late]))
    far_late = list(zip(places, pieces))
    terms = spread(both, 0)

    far_sum, *later = project(
        shard, far_late, far_gate, weights, proj_out, 0, main, extra, 0, None, partial, (both,)
    )
    if extra:
        far_sum = finish(later[0], last_gate, proj_out, main, far_sum, jnp.bfloat16, ())
    return score(terms, spread(far_sum, far), pairs)


def solution(mesh):
    return jax.shard_map(
        functools.partial(on_device, mesh.shape["dp"], mesh.shape["tensor"]),
        mesh=mesh,
        in_specs=(
            P(("parts", "dp"), "tensor"),
            P(("parts", "dp"), None, "tensor"),
            P(("parts", "dp"), "tensor"),
            P("tensor", "dp"),
            P("tensor", None),
            P("tensor", None),
            P("tensor", "dp"),
        ),
        out_specs=P("tensor", ("parts", "dp")),
        check_vma=False,
    )
```

```python
import functools

import jax
import jax.numpy as jnp
from jax import lax
from jax.experimental import pallas as pl
from jax.experimental.pallas import tpu as pltpu
from jax.sharding import PartitionSpec as P

TILE = 1024
SMALL = 512
RING = 4
VMEM = 60 * 1024 * 1024
ANY = pl.BlockSpec(memory_space=pl.ANY)


def swap(value, axis, size, mask):
    return lax.ppermute(value, axis, [(i, i ^ mask) for i in range(size)])


def split_kernel(first, grad_ref, *refs):
    me = lax.axis_index("dp")
    out_ref = refs[-1]
    blocks = [grad_ref[:, k, :] for k in range(grad_ref.shape[1])]
    bit = 1
    while bit < len(blocks):
        flip = (me & bit) != 0
        blocks = [jnp.where(flip, blocks[k ^ bit], blocks[k]) for k in range(len(blocks))]
        bit *= 2
    for k in range(out_ref.shape[0]):
        out_ref[k] = blocks[first + k].T


def split_blocks(out_grad, first, after):
    rows, n, width = out_grad.shape
    step = rows // 4
    return pl.pallas_call(
        functools.partial(split_kernel, first),
        grid=(4,),
        in_specs=[pl.BlockSpec((step, n, width), lambda i: (i, 0, 0))] + [ANY] * len(after),
        out_specs=pl.BlockSpec((n // 2, width, step), lambda i: (0, 0, i)),
        out_shape=jax.ShapeDtypeStruct((n // 2, width, rows), out_grad.dtype),
        compiler_params=pltpu.CompilerParams(vmem_limit_bytes=VMEM),
        name="split_blocks",
    )(out_grad, *after)


def gated(hidden, gate_ref, proj_ref):
    gate = gate_ref[...].T.astype(jnp.float32)
    silu = gate * (0.5 + 0.5 * jnp.tanh(0.5 * gate))
    up_grad = (hidden * silu).astype(jnp.bfloat16)
    return jnp.dot(proj_ref[...], up_grad, preferred_element_type=jnp.float32)


def project_kernel(tiles, ahead, pieces, chained, carried, shard_ref, *refs):
    refs = list(refs)
    take = lambda n: [refs.pop(0) for _ in range(n)]
    grads = take(pieces)
    weights = take(2 * pieces)
    gate_ref, proj_ref = take(2) if tiles else (None, None)
    (before_ref,) = take(1) if chained else (None,)
    (partial_ref,) = take(1) if carried else (None,)
    sum_ref, odd_ref, even_ref = [refs.pop() for _ in range(3)] if tiles else (None,) * 3
    later_ref = refs.pop() if ahead else None
    out_ref = refs.pop() if tiles else None
    step = pl.program_id(0)

    def multiply(hidden_ref):
        hidden = partial_ref[...] if carried else None
        for k, grad_ref in enumerate(grads):
            for p in range(2):
                term = jnp.dot(
                    weights[2 * k + p][...], grad_ref[p], preferred_element_type=jnp.float32
                )
                hidden = term if hidden is None else hidden + term
        hidden_ref[...] = hidden

    if not tiles:
        multiply(later_ref)
        return

    def reduce(hidden_ref):
        sum_ref[...] += gated(hidden_ref[...], gate_ref, proj_ref)

    @pl.when(step == 0)
    def _():
        sum_ref[...] = before_ref[...] if chained else jnp.zeros_like(sum_ref)
        multiply(even_ref)

    @pl.when((step > 0) & (step < tiles) & (lax.rem(step, 2) == 1))
    def _():
        reduce(even_ref)
        multiply(odd_ref)

    @pl.when((step > 0) & (step < tiles) & (lax.rem(step, 2) == 0))
    def _():
        reduce(odd_ref)
        multiply(even_ref)

    @pl.when(step == tiles)
    def _():
        reduce(even_ref if tiles % 2 else odd_ref)
        out_ref[...] = sum_ref[...]
        if ahead:
            multiply(later_ref)

    if ahead > 1:

        @pl.when(step > tiles)
        def _():
            multiply(later_ref)


def project(shard, grads, gate, weights, proj, offset, span, extra, gate_column, before, partial, after):
    places = [place for place, _ in grads]
    pieces = [piece for _, piece in grads]
    _, width, rows = pieces[0].shape
    count = weights[0].shape[1] // width
    k = proj.shape[0]
    tile = TILE if (span + extra) % TILE == 0 else span + extra
    tiles, ahead = span // tile, extra // tile
    first, gate_first = offset // tile, gate_column // tile
    now = lambda i: jnp.minimum(i, tiles + ahead - 1)
    last = lambda i: jnp.clip(i - 1, 0, max(tiles - 1, 0))
    chained, carried = before is not None, partial is not None
    total = pl.BlockSpec((k, rows), lambda i, s: (0, 0))
    later = pl.BlockSpec((tile, rows), lambda i, s: (jnp.maximum(i - tiles, 0), 0))

    def weight_spec(place):
        return pl.BlockSpec(
            (tile, width), lambda i, s: (first + now(i), lax.rem(s[0] + count - place, count))
        )

    specs = [pl.BlockSpec((2, width, rows), lambda i, s: (0, 0, 0)) for _ in pieces]
    specs += [weight_spec(place) for place in places for _ in range(2)]
    operands = pieces + [weight for _ in places for weight in weights]
    if tiles:
        specs += [
            pl.BlockSpec((rows, tile), lambda i, s: (0, gate_first + last(i))),
            pl.BlockSpec((k, tile), lambda i, s: (0, first + last(i))),
        ]
        operands += [gate, proj]
    if chained:
        specs.append(total)
        operands.append(before)
    if carried:
        specs.append(pl.BlockSpec((tile, rows), lambda i, s: (first + now(i), 0)))
        operands.append(partial)
    hidden = pltpu.VMEM((tile, rows), jnp.float32)
    depth = 2 * width * len(pieces)
    return pl.pallas_call(
        functools.partial(project_kernel, tiles, ahead, len(pieces), chained, carried),
        grid_spec=pltpu.PrefetchScalarGridSpec(
            num_scalar_prefetch=1,
            grid=(tiles + max(ahead, 1) if tiles else ahead,),
            in_specs=specs + [ANY] * len(after),
            out_specs=[total] * bool(tiles) + [later] * bool(ahead),
            scratch_shapes=[hidden, hidden, pltpu.VMEM((k, rows), jnp.float32)] if tiles else [],
        ),
        out_shape=[jax.ShapeDtypeStruct((k, rows), jnp.float32)] * bool(tiles)
        + [jax.ShapeDtypeStruct((extra, rows), jnp.float32)] * bool(ahead),
        compiler_params=pltpu.CompilerParams(vmem_limit_bytes=VMEM),
        cost_estimate=pl.CostEstimate(
            flops=2 * rows * (span + extra) * depth,
            bytes_accessed=2 * (span + extra) * (depth + rows),
            transcendentals=rows * span,
        ),
        name="project",
    )(shard, *operands, *after)


def finish_kernel(hidden_ref, gate_ref, proj_ref, before_ref, *refs):
    out_ref, sum_ref = refs[-2:]
    part = gated(hidden_ref[...], gate_ref, proj_ref)

    @pl.when(pl.program_id(0) == 0)
    def _():
        sum_ref[...] = before_ref[...] + part

    @pl.when(pl.program_id(0) > 0)
    def _():
        sum_ref[...] += part

    @pl.when(pl.program_id(0) == pl.num_programs(0) - 1)
    def _():
        out_ref[...] = sum_ref[...].astype(out_ref.dtype)


def finish(hidden, row, gate, proj, offset, before, dtype, after):
    rows, span = gate.shape
    k = proj.shape[0]
    start, first = row // SMALL, offset // SMALL
    total = pl.BlockSpec((k, rows), lambda i: (0, 0))
    return pl.pallas_call(
        finish_kernel,
        grid=(span // SMALL,),
        in_specs=[
            pl.BlockSpec((SMALL, rows), lambda i: (start + i, 0)),
            pl.BlockSpec((rows, SMALL), lambda i: (0, i)),
            pl.BlockSpec((k, SMALL), lambda i: (0, first + i)),
            total,
        ]
        + [ANY] * len(after),
        out_specs=total,
        out_shape=jax.ShapeDtypeStruct((k, rows), dtype),
        scratch_shapes=[pltpu.VMEM((k, rows), jnp.float32)],
        compiler_params=pltpu.CompilerParams(vmem_limit_bytes=VMEM),
        name="finish",
    )(hidden, gate, proj, before, *after)


def score_kernel(n_both, parts, out_ref):
    *parts, query_ref = parts
    total = lambda refs: functools.reduce(jnp.add, [ref[...].astype(jnp.float32) for ref in refs])
    grad = total(parts[n_both:])
    inputs, own = jnp.split(total(parts[:n_both]), 2)
    grad += own
    high = grad.astype(jnp.bfloat16)
    low = (grad - high.astype(jnp.float32)).astype(jnp.bfloat16)
    both = jnp.concatenate([high, low], axis=0)
    count = out_ref.shape[0]
    k = inputs.shape[0]
    group = 8
    scores = jnp.zeros(out_ref.shape, jnp.float32)
    for i in range(0, k, group):
        part = jnp.dot(
            query_ref[i * count : (i + group) * count, :], both, preferred_element_type=jnp.float32
        )
        for n in range(group):
            scores += inputs[i + n : i + n + 1, :] * part[n * count : (n + 1) * count, :]
    out_ref[...] = scores


def pair_queries(queries, k):
    pairs = queries.reshape(queries.shape[0], k, k).transpose(1, 0, 2).reshape(-1, k)
    return jnp.concatenate([pairs, pairs], axis=1)


def score(both, grads, pairs):
    k, rows = grads[0].shape
    return pl.pallas_call(
        lambda *refs: score_kernel(len(both), refs[:-1], refs[-1]),
        out_shape=jax.ShapeDtypeStruct((pairs.shape[0] // k, rows), jnp.float32),
        compiler_params=pltpu.CompilerParams(vmem_limit_bytes=VMEM),
        name="score",
    )(*both, *grads, pairs)


def chunks_of(hidden):
    units = hidden // TILE
    if hidden % TILE or units < 4:
        return hidden, 0, 0
    return hidden - 2 * TILE, TILE, TILE


def on_device(n_dp, n_tensor, inputs, out_grad, gate_pre, down_weight, proj_in, proj_out, queries):
    rows = out_grad.shape[0]
    hidden = gate_pre.shape[1]
    me = lax.axis_index("dp")
    shard = lax.axis_index("tensor").astype(jnp.int32).reshape(1)
    far, near = n_dp // 2, 1
    ring = n_tensor <= RING
    main, last, start = chunks_of(hidden)

    def onward(piece, hold=None):
        if hold is not None:
            piece, _ = lax.optimization_barrier((piece, hold))
        return lax.ppermute(piece, "tensor", [(i, (i + 1) % n_tensor) for i in range(n_tensor)])

    def gather(block):
        grad = lax.all_gather(block, "tensor", axis=0, tiled=False)
        return jnp.transpose(grad, (1, 0, 2, 3)).reshape(2, -1, rows)

    def spread(value, mask):
        if not ring:
            total = lax.psum(value.astype(jnp.float32), "tensor")
            return [swap(total, "dp", n_dp, mask) if mask else total]
        got = [value] if not mask else []
        for step in range(0 if mask else 1, n_tensor):
            pairs = [
                (z * n_dp + d, (z + step) % n_tensor * n_dp + (d ^ mask))
                for z in range(n_tensor)
                for d in range(n_dp)
            ]
            got.append(lax.ppermute(value, ("tensor", "dp"), pairs))
        return got

    weights = (down_weight, swap(down_weight, "dp", n_dp, near))
    far_query = swap(queries, "dp", n_dp, far)

    start_gate = gate_pre[:, main + last :]
    own_blocks = split_blocks(out_grad, 0, (start_gate,) if start else ())
    far_blocks = split_blocks(out_grad, n_dp // 2, (own_blocks,))
    far_blocks, _ = lax.optimization_barrier((far_blocks, far_query))
    far_start = swap(far_blocks, "dp", n_dp, far)
    own = [own_blocks, onward(own_blocks)] if ring and n_tensor > 1 else [own_blocks]
    if start:
        start_gate = swap(start_gate, "dp", n_dp, far)
    gates, far_start, start_gate, _ = lax.optimization_barrier(
        ((gate_pre[:, :main], gate_pre[:, main : main + last]), far_start, start_gate, own[-1])
    )
    far_gate, last_gate = (swap(part, "dp", n_dp, far) if part.size else None for part in gates)

    def all_pairs(hold):
        blocks, _ = lax.optimization_barrier(((queries, far_query), hold))
        blocks += tuple(swap(block, "dp", n_dp, near) for block in blocks)
        width = queries.shape[1]
        merged = jnp.zeros((queries.shape[0], n_dp * width), queries.dtype)
        for mask, block in zip((0, far, near, far ^ near), blocks):
            merged = lax.dynamic_update_slice(merged, block, (0, (me ^ mask) * width))
        return pair_queries(merged, proj_in.shape[1])

    proj_out = proj_out.T
    if ring and n_tensor > 1:
        split = n_tensor // 2
        while len(own) <= split:
            own.append(onward(own[-1]))
        own_early = list(enumerate(own))[:split]
        (own_sum,) = project(
            shard, own_early, gate_pre, weights, proj_out, 0, hidden, 0, 0, None, None, (own[-1],)
        )
        early_sum = own_sum
        pairs = all_pairs(early_sum)
        others = [far_start]
        for _ in range(split - 1):
            others.append(onward(others[-1]))
        far_early = list(enumerate(others))
        (partial,) = project(
            shard, far_early, None, weights, proj_out, 0, 0, hidden, 0, None, None, (own_sum,)
        )
        while len(own) < n_tensor:
            own.append(onward(own[-1], early_sum))
        own_late = list(enumerate(own))[split:]
        middle = -(-hidden // (2 * TILE)) * TILE if hidden % TILE == 0 else hidden
        after = (partial,)
        for s in range(0, hidden, middle):
            span = min(middle, hidden - s)
            (own_sum,) = project(
                shard, own_late, gate_pre, weights, proj_out, s, span, 0, s, own_sum, None, after
            )
            if s == 0:
                while len(others) < n_tensor:
                    hold = own_sum if len(others) == n_tensor - 1 else early_sum
                    others.append(onward(others[-1], hold))
            after = (pairs,)
        far_late = list(enumerate(others))[split:]
    else:
        (own_sum,) = project(
            shard, [(0, gather(own_blocks))], gate_pre, weights, proj_out, 0, hidden, 0, 0, None, None, ()
        )
        far_late, partial = [(0, gather(far_start))], None
        pairs = all_pairs(own_sum)

    input_part = lax.dot_general(
        proj_in, inputs, (((0,), (1,)), ((), ())), preferred_element_type=jnp.float32
    )
    both = jnp.concatenate([input_part, own_sum])
    both, far_gate = lax.optimization_barrier((both, far_gate))
    terms = spread(both, 0)

    far_sum, *later = project(
        shard, far_late, far_gate, weights, proj_out, 0, main, last + start, 0, None, partial, (both,)
    )
    if later:
        far_sum = finish(
            later[0], last, start_gate, proj_out, main + last, far_sum, jnp.float32, ()
        )
        far_sum = finish(
            later[0], 0, last_gate, proj_out, main, far_sum, jnp.bfloat16, tuple(terms[1:])
        )
    return score(terms, spread(far_sum, far), pairs)


def solution(mesh):
    return jax.shard_map(
        functools.partial(on_device, mesh.shape["dp"], mesh.shape["tensor"]),
        mesh=mesh,
        in_specs=(
            P(("parts", "dp"), "tensor"),
            P(("parts", "dp"), None, "tensor"),
            P(("parts", "dp"), "tensor"),
            P("tensor", "dp"),
            P("tensor", None),
            P("tensor", None),
            P("tensor", "dp"),
        ),
        out_specs=P("tensor", ("parts", "dp")),
        check_vma=False,
    )
```

```python
import functools

import jax
import jax.numpy as jnp
from jax import lax
from jax.experimental import pallas as pl
from jax.experimental.pallas import tpu as pltpu
from jax.sharding import PartitionSpec as P

TILE = 1024
SMALL = 512
RING = 4
VMEM = 60 * 1024 * 1024
ANY = pl.BlockSpec(memory_space=pl.ANY)


def swap(value, axis, size, mask):
    return lax.ppermute(value, axis, [(i, i ^ mask) for i in range(size)])


def split_kernel(first, grad_ref, *refs):
    me = lax.axis_index("dp")
    out_ref = refs[-1]
    blocks = [grad_ref[:, k, :] for k in range(grad_ref.shape[1])]
    bit = 1
    while bit < len(blocks):
        flip = (me & bit) != 0
        blocks = [jnp.where(flip, blocks[k ^ bit], blocks[k]) for k in range(len(blocks))]
        bit *= 2
    for k in range(out_ref.shape[0]):
        out_ref[k] = blocks[first + k].T


def split_blocks(out_grad, first, after):
    rows, n, width = out_grad.shape
    step = rows // 4
    return pl.pallas_call(
        functools.partial(split_kernel, first),
        grid=(4,),
        in_specs=[pl.BlockSpec((step, n, width), lambda i: (i, 0, 0))] + [ANY] * len(after),
        out_specs=pl.BlockSpec((n // 2, width, step), lambda i: (0, 0, i)),
        out_shape=jax.ShapeDtypeStruct((n // 2, width, rows), out_grad.dtype),
        compiler_params=pltpu.CompilerParams(vmem_limit_bytes=VMEM),
        name="split_blocks",
    )(out_grad, *after)


def gated(hidden, gate_ref, proj_ref):
    gate = gate_ref[...].T.astype(jnp.float32)
    silu = gate * (0.5 + 0.5 * jnp.tanh(0.5 * gate))
    up_grad = (hidden * silu).astype(jnp.bfloat16)
    return jnp.dot(proj_ref[...], up_grad, preferred_element_type=jnp.float32)


def project_kernel(tiles, ahead, pieces, chained, carried, shard_ref, *refs):
    refs = list(refs)
    take = lambda n: [refs.pop(0) for _ in range(n)]
    grads = take(pieces)
    weights = take(2 * pieces)
    gate_ref, proj_ref = take(2) if tiles else (None, None)
    (before_ref,) = take(1) if chained else (None,)
    (partial_ref,) = take(1) if carried else (None,)
    sum_ref, odd_ref, even_ref = [refs.pop() for _ in range(3)] if tiles else (None,) * 3
    later_ref = refs.pop() if ahead else None
    out_ref = refs.pop() if tiles else None
    step = pl.program_id(0)

    def multiply(hidden_ref):
        hidden = partial_ref[...] if carried else None
        for k, grad_ref in enumerate(grads):
            for p in range(2):
                term = jnp.dot(
                    weights[2 * k + p][...], grad_ref[p], preferred_element_type=jnp.float32
                )
                hidden = term if hidden is None else hidden + term
        hidden_ref[...] = hidden

    if not tiles:
        multiply(later_ref)
        return

    def reduce(hidden_ref):
        sum_ref[...] += gated(hidden_ref[...], gate_ref, proj_ref)

    @pl.when(step == 0)
    def _():
        sum_ref[...] = before_ref[...] if chained else jnp.zeros_like(sum_ref)
        multiply(even_ref)

    @pl.when((step > 0) & (step < tiles) & (lax.rem(step, 2) == 1))
    def _():
        reduce(even_ref)
        multiply(odd_ref)

    @pl.when((step > 0) & (step < tiles) & (lax.rem(step, 2) == 0))
    def _():
        reduce(odd_ref)
        multiply(even_ref)

    @pl.when(step == tiles)
    def _():
        reduce(even_ref if tiles % 2 else odd_ref)
        out_ref[...] = sum_ref[...]
        if ahead:
            multiply(later_ref)

    if ahead > 1:

        @pl.when(step > tiles)
        def _():
            multiply(later_ref)


def project(shard, grads, gate, weights, proj, offset, span, extra, gate_column, before, partial, after):
    places = [place for place, _ in grads]
    pieces = [piece for _, piece in grads]
    _, width, rows = pieces[0].shape
    count = weights[0].shape[1] // width
    k = proj.shape[0]
    tile = TILE if (span + extra) % TILE == 0 else span + extra
    tiles, ahead = span // tile, extra // tile
    first, gate_first = offset // tile, gate_column // tile
    now = lambda i: jnp.minimum(i, tiles + ahead - 1)
    last = lambda i: jnp.clip(i - 1, 0, max(tiles - 1, 0))
    chained, carried = before is not None, partial is not None
    total = pl.BlockSpec((k, rows), lambda i, s: (0, 0))
    later = pl.BlockSpec((tile, rows), lambda i, s: (jnp.maximum(i - tiles, 0), 0))

    def weight_spec(place):
        return pl.BlockSpec(
            (tile, width), lambda i, s: (first + now(i), lax.rem(s[0] + count - place, count))
        )

    specs = [pl.BlockSpec((2, width, rows), lambda i, s: (0, 0, 0)) for _ in pieces]
    specs += [weight_spec(place) for place in places for _ in range(2)]
    operands = pieces + [weight for _ in places for weight in weights]
    if tiles:
        specs += [
            pl.BlockSpec((rows, tile), lambda i, s: (0, gate_first + last(i))),
            pl.BlockSpec((k, tile), lambda i, s: (0, first + last(i))),
        ]
        operands += [gate, proj]
    if chained:
        specs.append(total)
        operands.append(before)
    if carried:
        specs.append(pl.BlockSpec((tile, rows), lambda i, s: (first + now(i), 0)))
        operands.append(partial)
    hidden = pltpu.VMEM((tile, rows), jnp.float32)
    depth = 2 * width * len(pieces)
    return pl.pallas_call(
        functools.partial(project_kernel, tiles, ahead, len(pieces), chained, carried),
        grid_spec=pltpu.PrefetchScalarGridSpec(
            num_scalar_prefetch=1,
            grid=(tiles + max(ahead, 1) if tiles else ahead,),
            in_specs=specs + [ANY] * len(after),
            out_specs=[total] * bool(tiles) + [later] * bool(ahead),
            scratch_shapes=[hidden, hidden, pltpu.VMEM((k, rows), jnp.float32)] if tiles else [],
        ),
        out_shape=[jax.ShapeDtypeStruct((k, rows), jnp.float32)] * bool(tiles)
        + [jax.ShapeDtypeStruct((extra, rows), jnp.float32)] * bool(ahead),
        compiler_params=pltpu.CompilerParams(vmem_limit_bytes=VMEM),
        cost_estimate=pl.CostEstimate(
            flops=2 * rows * (span + extra) * depth,
            bytes_accessed=2 * (span + extra) * (depth + rows),
            transcendentals=rows * span,
        ),
        name="project",
    )(shard, *operands, *after)


def finish_kernel(hidden_ref, gate_ref, proj_ref, before_ref, *refs):
    out_ref, sum_ref = refs[-2:]
    part = gated(hidden_ref[...], gate_ref, proj_ref)

    @pl.when(pl.program_id(0) == 0)
    def _():
        sum_ref[...] = before_ref[...] + part

    @pl.when(pl.program_id(0) > 0)
    def _():
        sum_ref[...] += part

    @pl.when(pl.program_id(0) == pl.num_programs(0) - 1)
    def _():
        out_ref[...] = sum_ref[...].astype(out_ref.dtype)


def finish(hidden, row, gate, proj, offset, before, dtype, after):
    rows, span = gate.shape
    k = proj.shape[0]
    start, first = row // SMALL, offset // SMALL
    total = pl.BlockSpec((k, rows), lambda i: (0, 0))
    return pl.pallas_call(
        finish_kernel,
        grid=(span // SMALL,),
        in_specs=[
            pl.BlockSpec((SMALL, rows), lambda i: (start + i, 0)),
            pl.BlockSpec((rows, SMALL), lambda i: (0, i)),
            pl.BlockSpec((k, SMALL), lambda i: (0, first + i)),
            total,
        ]
        + [ANY] * len(after),
        out_specs=total,
        out_shape=jax.ShapeDtypeStruct((k, rows), dtype),
        scratch_shapes=[pltpu.VMEM((k, rows), jnp.float32)],
        compiler_params=pltpu.CompilerParams(vmem_limit_bytes=VMEM),
        name="finish",
    )(hidden, gate, proj, before, *after)


def score_kernel(n_both, parts, out_ref):
    *parts, query_ref = parts
    total = lambda refs: functools.reduce(jnp.add, [ref[...].astype(jnp.float32) for ref in refs])
    grad = total(parts[n_both:])
    inputs, own = jnp.split(total(parts[:n_both]), 2)
    grad += own
    high = grad.astype(jnp.bfloat16)
    low = (grad - high.astype(jnp.float32)).astype(jnp.bfloat16)
    both = jnp.concatenate([high, low], axis=0)
    count = out_ref.shape[0]
    k = inputs.shape[0]
    group = 8
    scores = jnp.zeros(out_ref.shape, jnp.float32)
    for i in range(0, k, group):
        part = jnp.dot(
            query_ref[i * count : (i + group) * count, :], both, preferred_element_type=jnp.float32
        )
        for n in range(group):
            scores += inputs[i + n : i + n + 1, :] * part[n * count : (n + 1) * count, :]
    out_ref[...] = scores


def pair_queries(queries, k):
    pairs = queries.reshape(queries.shape[0], k, k).transpose(1, 0, 2).reshape(-1, k)
    return jnp.concatenate([pairs, pairs], axis=1)


def score(both, grads, pairs):
    k, rows = grads[0].shape
    return pl.pallas_call(
        lambda *refs: score_kernel(len(both), refs[:-1], refs[-1]),
        out_shape=jax.ShapeDtypeStruct((pairs.shape[0] // k, rows), jnp.float32),
        compiler_params=pltpu.CompilerParams(vmem_limit_bytes=VMEM),
        name="score",
    )(*both, *grads, pairs)


def chunks_of(hidden):
    units = hidden // TILE
    if hidden % TILE or units < 5:
        return hidden, []
    return hidden - 3 * TILE, [TILE] * 3


def on_device(n_dp, n_tensor, inputs, out_grad, gate_pre, down_weight, proj_in, proj_out, queries):
    rows = out_grad.shape[0]
    hidden = gate_pre.shape[1]
    me = lax.axis_index("dp")
    shard = lax.axis_index("tensor").astype(jnp.int32).reshape(1)
    far, near = n_dp // 2, 1
    ring = n_tensor <= RING
    main, spans = chunks_of(hidden)
    offsets = [main + sum(spans[:k]) for k in range(len(spans))]

    def onward(piece, hold=None):
        if hold is not None:
            piece, _ = lax.optimization_barrier((piece, hold))
        return lax.ppermute(piece, "tensor", [(i, (i + 1) % n_tensor) for i in range(n_tensor)])

    def gather(block):
        grad = lax.all_gather(block, "tensor", axis=0, tiled=False)
        return jnp.transpose(grad, (1, 0, 2, 3)).reshape(2, -1, rows)

    def spread(value, mask):
        if not ring:
            total = lax.psum(value.astype(jnp.float32), "tensor")
            return [swap(total, "dp", n_dp, mask) if mask else total]
        got = [value] if not mask else []
        for step in range(0 if mask else 1, n_tensor):
            pairs = [
                (z * n_dp + d, (z + step) % n_tensor * n_dp + (d ^ mask))
                for z in range(n_tensor)
                for d in range(n_dp)
            ]
            got.append(lax.ppermute(value, ("tensor", "dp"), pairs))
        return got

    weights = (down_weight, swap(down_weight, "dp", n_dp, near))
    far_query = swap(queries, "dp", n_dp, far)

    cut = lambda source, offset, span: source[:, offset : offset + span]
    start_gate = cut(gate_pre, offsets[-1], spans[-1]) if spans else None
    own_blocks = split_blocks(out_grad, 0, (start_gate,) if spans else ())
    far_blocks = split_blocks(out_grad, n_dp // 2, (own_blocks,))
    if spans:
        start_gate = swap(start_gate, "dp", n_dp, far)
    far_blocks, start_gate, _ = lax.optimization_barrier((far_blocks, start_gate, far_query))
    far_start = swap(far_blocks, "dp", n_dp, far)
    own = [own_blocks, onward(own_blocks)] if ring and n_tensor > 1 else [own_blocks]
    later_gate, _ = lax.optimization_barrier((gate_pre, own_blocks))
    parts = [cut(later_gate, 0, main)]
    parts += [cut(later_gate, offset, span) for offset, span in zip(offsets[:-1], spans)]
    parts, far_start, _ = lax.optimization_barrier((parts, far_start, own[-1]))
    far_gate, *last_gates = [swap(part, "dp", n_dp, far) for part in parts]

    def all_pairs(hold):
        blocks, _ = lax.optimization_barrier(((queries, far_query), hold))
        blocks += tuple(swap(block, "dp", n_dp, near) for block in blocks)
        width = queries.shape[1]
        merged = jnp.zeros((queries.shape[0], n_dp * width), queries.dtype)
        for mask, block in zip((0, far, near, far ^ near), blocks):
            merged = lax.dynamic_update_slice(merged, block, (0, (me ^ mask) * width))
        return pair_queries(merged, proj_in.shape[1])

    proj_out = proj_out.T
    if ring and n_tensor > 1:
        split = n_tensor // 2
        while len(own) <= split:
            own.append(onward(own[-1]))
        own_early = list(enumerate(own))[:split]
        (own_sum,) = project(
            shard, own_early, gate_pre, weights, proj_out, 0, hidden, 0, 0, None, None, (own[-1],)
        )
        early_sum = own_sum
        pairs = all_pairs(early_sum)
        others = [far_start]
        for _ in range(split - 1):
            others.append(onward(others[-1]))
        far_early = list(enumerate(others))
        (partial,) = project(
            shard, far_early, None, weights, proj_out, 0, 0, hidden, 0, None, None, (own_sum,)
        )
        while len(own) < n_tensor:
            own.append(onward(own[-1], early_sum))
        own_late = list(enumerate(own))[split:]
        middle = -(-hidden // (2 * TILE)) * TILE if hidden % TILE == 0 else hidden
        after = (partial,)
        for s in range(0, hidden, middle):
            span = min(middle, hidden - s)
            (own_sum,) = project(
                shard, own_late, gate_pre, weights, proj_out, s, span, 0, s, own_sum, None, after
            )
            if s == 0:
                while len(others) < n_tensor:
                    hold = own_sum if len(others) == n_tensor - 1 else early_sum
                    others.append(onward(others[-1], hold))
            after = (pairs,)
        far_late = list(enumerate(others))[split:]
    else:
        (own_sum,) = project(
            shard, [(0, gather(own_blocks))], gate_pre, weights, proj_out, 0, hidden, 0, 0, None, None, ()
        )
        far_late, partial = [(0, gather(far_start))], None
        pairs = all_pairs(own_sum)

    input_part = lax.dot_general(
        proj_in, inputs, (((0,), (1,)), ((), ())), preferred_element_type=jnp.float32
    )
    both = jnp.concatenate([input_part, own_sum])
    both, far_gate = lax.optimization_barrier((both, far_gate))
    terms = spread(both, 0)

    far_sum, *later = project(
        shard, far_late, far_gate, weights, proj_out, 0, main, sum(spans), 0, None, partial, (both,)
    )
    if later:
        order = [len(spans) - 1] + list(range(len(spans) - 1))
        for k, gate in zip(order, [start_gate] + last_gates):
            final = k == order[-1]
            far_sum = finish(
                later[0],
                offsets[k] - main,
                gate,
                proj_out,
                offsets[k],
                far_sum,
                jnp.bfloat16 if final else jnp.float32,
                tuple(terms[1:]) if final else (),
            )
    return score(terms, spread(far_sum, far), pairs)


def solution(mesh):
    return jax.shard_map(
        functools.partial(on_device, mesh.shape["dp"], mesh.shape["tensor"]),
        mesh=mesh,
        in_specs=(
            P(("parts", "dp"), "tensor"),
            P(("parts", "dp"), None, "tensor"),
            P(("parts", "dp"), "tensor"),
            P("tensor", "dp"),
            P("tensor", None),
            P("tensor", None),
            P("tensor", "dp"),
        ),
        out_specs=P("tensor", ("parts", "dp")),
        check_vma=False,
    )
```

```python
import functools

import jax
import jax.numpy as jnp
from jax import lax
from jax.experimental import pallas as pl
from jax.experimental.pallas import tpu as pltpu
from jax.sharding import PartitionSpec as P

TILE = 1024
SMALL = 512
RING = 4
VMEM = 60 * 1024 * 1024
ANY = pl.BlockSpec(memory_space=pl.ANY)


def swap(value, axis, size, mask):
    return lax.ppermute(value, axis, [(i, i ^ mask) for i in range(size)])


def split_kernel(first, grad_ref, *refs):
    me = lax.axis_index("dp")
    out_ref = refs[-1]
    blocks = [grad_ref[:, k, :] for k in range(grad_ref.shape[1])]
    bit = 1
    while bit < len(blocks):
        flip = (me & bit) != 0
        blocks = [jnp.where(flip, blocks[k ^ bit], blocks[k]) for k in range(len(blocks))]
        bit *= 2
    for k in range(out_ref.shape[0]):
        out_ref[k] = blocks[first + k].T


def split_blocks(out_grad, first, after):
    rows, n, width = out_grad.shape
    step = rows // 4
    return pl.pallas_call(
        functools.partial(split_kernel, first),
        grid=(4,),
        in_specs=[pl.BlockSpec((step, n, width), lambda i: (i, 0, 0))] + [ANY] * len(after),
        out_specs=pl.BlockSpec((n // 2, width, step), lambda i: (0, 0, i)),
        out_shape=jax.ShapeDtypeStruct((n // 2, width, rows), out_grad.dtype),
        compiler_params=pltpu.CompilerParams(vmem_limit_bytes=VMEM),
        name="split_blocks",
    )(out_grad, *after)


def gated(hidden, gate_ref, proj_ref):
    gate = gate_ref[...].T.astype(jnp.float32)
    silu = gate * (0.5 + 0.5 * jnp.tanh(0.5 * gate))
    up_grad = (hidden * silu).astype(jnp.bfloat16)
    return jnp.dot(proj_ref[...], up_grad, preferred_element_type=jnp.float32)


def project_kernel(tiles, ahead, pieces, chained, carried, shard_ref, *refs):
    refs = list(refs)
    take = lambda n: [refs.pop(0) for _ in range(n)]
    grads = take(pieces)
    weights = take(2 * pieces)
    gate_ref, proj_ref = take(2) if tiles else (None, None)
    (before_ref,) = take(1) if chained else (None,)
    (partial_ref,) = take(1) if carried else (None,)
    sum_ref, odd_ref, even_ref = [refs.pop() for _ in range(3)] if tiles else (None,) * 3
    later_ref = refs.pop() if ahead else None
    out_ref = refs.pop() if tiles else None
    step = pl.program_id(0)

    def multiply(hidden_ref):
        hidden = partial_ref[...] if carried else None
        for k, grad_ref in enumerate(grads):
            for p in range(2):
                term = jnp.dot(
                    weights[2 * k + p][...], grad_ref[p], preferred_element_type=jnp.float32
                )
                hidden = term if hidden is None else hidden + term
        hidden_ref[...] = hidden

    if not tiles:
        multiply(later_ref)
        return

    def reduce(hidden_ref):
        sum_ref[...] += gated(hidden_ref[...], gate_ref, proj_ref)

    @pl.when(step == 0)
    def _():
        sum_ref[...] = before_ref[...] if chained else jnp.zeros_like(sum_ref)
        multiply(even_ref)

    @pl.when((step > 0) & (step < tiles) & (lax.rem(step, 2) == 1))
    def _():
        reduce(even_ref)
        multiply(odd_ref)

    @pl.when((step > 0) & (step < tiles) & (lax.rem(step, 2) == 0))
    def _():
        reduce(odd_ref)
        multiply(even_ref)

    @pl.when(step == tiles)
    def _():
        reduce(even_ref if tiles % 2 else odd_ref)
        out_ref[...] = sum_ref[...]
        if ahead:
            multiply(later_ref)

    if ahead > 1:

        @pl.when(step > tiles)
        def _():
            multiply(later_ref)


def project(shard, grads, gate, weights, proj, offset, span, extra, gate_column, before, partial, after):
    places = [place for place, _ in grads]
    pieces = [piece for _, piece in grads]
    _, width, rows = pieces[0].shape
    count = weights[0].shape[1] // width
    k = proj.shape[0]
    tile = TILE if (span + extra) % TILE == 0 else span + extra
    tiles, ahead = span // tile, extra // tile
    first, gate_first = offset // tile, gate_column // tile
    now = lambda i: jnp.minimum(i, tiles + ahead - 1)
    last = lambda i: jnp.clip(i - 1, 0, max(tiles - 1, 0))
    chained, carried = before is not None, partial is not None
    total = pl.BlockSpec((k, rows), lambda i, s: (0, 0))
    later = pl.BlockSpec((tile, rows), lambda i, s: (jnp.maximum(i - tiles, 0), 0))

    def weight_spec(place):
        return pl.BlockSpec(
            (tile, width), lambda i, s: (first + now(i), lax.rem(s[0] + count - place, count))
        )

    specs = [pl.BlockSpec((2, width, rows), lambda i, s: (0, 0, 0)) for _ in pieces]
    specs += [weight_spec(place) for place in places for _ in range(2)]
    operands = pieces + [weight for _ in places for weight in weights]
    if tiles:
        specs += [
            pl.BlockSpec((rows, tile), lambda i, s: (0, gate_first + last(i))),
            pl.BlockSpec((k, tile), lambda i, s: (0, first + last(i))),
        ]
        operands += [gate, proj]
    if chained:
        specs.append(total)
        operands.append(before)
    if carried:
        specs.append(pl.BlockSpec((tile, rows), lambda i, s: (first + now(i), 0)))
        operands.append(partial)
    hidden = pltpu.VMEM((tile, rows), jnp.float32)
    depth = 2 * width * len(pieces)
    return pl.pallas_call(
        functools.partial(project_kernel, tiles, ahead, len(pieces), chained, carried),
        grid_spec=pltpu.PrefetchScalarGridSpec(
            num_scalar_prefetch=1,
            grid=(tiles + max(ahead, 1) if tiles else ahead,),
            in_specs=specs + [ANY] * len(after),
            out_specs=[total] * bool(tiles) + [later] * bool(ahead),
            scratch_shapes=[hidden, hidden, pltpu.VMEM((k, rows), jnp.float32)] if tiles else [],
        ),
        out_shape=[jax.ShapeDtypeStruct((k, rows), jnp.float32)] * bool(tiles)
        + [jax.ShapeDtypeStruct((extra, rows), jnp.float32)] * bool(ahead),
        compiler_params=pltpu.CompilerParams(vmem_limit_bytes=VMEM),
        cost_estimate=pl.CostEstimate(
            flops=2 * rows * (span + extra) * depth,
            bytes_accessed=2 * (span + extra) * (depth + rows),
            transcendentals=rows * span,
        ),
        name="project",
    )(shard, *operands, *after)


def finish_kernel(hidden_ref, gate_ref, proj_ref, before_ref, *refs):
    out_ref, sum_ref = refs[-2:]
    part = gated(hidden_ref[...], gate_ref, proj_ref)

    @pl.when(pl.program_id(0) == 0)
    def _():
        sum_ref[...] = before_ref[...] + part

    @pl.when(pl.program_id(0) > 0)
    def _():
        sum_ref[...] += part

    @pl.when(pl.program_id(0) == pl.num_programs(0) - 1)
    def _():
        out_ref[...] = sum_ref[...].astype(out_ref.dtype)


def finish(hidden, row, gate, proj, offset, before, dtype, after):
    rows, span = gate.shape
    k = proj.shape[0]
    start, first = row // SMALL, offset // SMALL
    total = pl.BlockSpec((k, rows), lambda i: (0, 0))
    return pl.pallas_call(
        finish_kernel,
        grid=(span // SMALL,),
        in_specs=[
            pl.BlockSpec((SMALL, rows), lambda i: (start + i, 0)),
            pl.BlockSpec((rows, SMALL), lambda i: (0, i)),
            pl.BlockSpec((k, SMALL), lambda i: (0, first + i)),
            total,
        ]
        + [ANY] * len(after),
        out_specs=total,
        out_shape=jax.ShapeDtypeStruct((k, rows), dtype),
        scratch_shapes=[pltpu.VMEM((k, rows), jnp.float32)],
        compiler_params=pltpu.CompilerParams(vmem_limit_bytes=VMEM),
        name="finish",
    )(hidden, gate, proj, before, *after)


def score_kernel(n_both, *refs):
    *parts, query_ref, out_ref = refs
    both = functools.reduce(jnp.add, [ref[...] for ref in parts[:n_both]])
    inputs, grad = jnp.split(both, 2)
    for part_ref in parts[n_both:]:
        grad += part_ref[...].astype(jnp.float32)
    high = grad.astype(jnp.bfloat16)
    low = (grad - high.astype(jnp.float32)).astype(jnp.bfloat16)
    both = jnp.concatenate([high, low], axis=0)
    count = out_ref.shape[0]
    k = inputs.shape[0]
    group = 8
    scores = jnp.zeros(out_ref.shape, jnp.float32)
    for i in range(0, k, group):
        part = jnp.dot(
            query_ref[i * count : (i + group) * count, :], both, preferred_element_type=jnp.float32
        )
        for n in range(group):
            scores += inputs[i + n : i + n + 1, :] * part[n * count : (n + 1) * count, :]
    out_ref[...] = scores


def pair_queries(queries, k):
    pairs = queries.reshape(queries.shape[0], k, k).transpose(1, 0, 2).reshape(-1, k)
    return jnp.concatenate([pairs, pairs], axis=1)


def score(both, grads, pairs):
    k, rows = grads[0].shape
    return pl.pallas_call(
        functools.partial(score_kernel, len(both)),
        out_shape=jax.ShapeDtypeStruct((pairs.shape[0] // k, rows), jnp.float32),
        compiler_params=pltpu.CompilerParams(vmem_limit_bytes=VMEM),
        name="score",
    )(*both, *grads, pairs)


def chunks_of(hidden):
    units = hidden // TILE
    if hidden % TILE or units < 5:
        return hidden, []
    return hidden - 3 * TILE, [2 * TILE - SMALL, SMALL, TILE]


def on_device(n_dp, n_tensor, inputs, out_grad, gate_pre, down_weight, proj_in, proj_out, queries):
    rows = out_grad.shape[0]
    hidden = gate_pre.shape[1]
    me = lax.axis_index("dp")
    shard = lax.axis_index("tensor").astype(jnp.int32).reshape(1)
    far, near = n_dp // 2, 1
    ring = n_tensor <= RING
    main, spans = chunks_of(hidden)
    offsets = [main + sum(spans[:k]) for k in range(len(spans))]

    def onward(piece, hold=None):
        if hold is not None:
            piece, _ = lax.optimization_barrier((piece, hold))
        return lax.ppermute(piece, "tensor", [(i, (i + 1) % n_tensor) for i in range(n_tensor)])

    def gather(block):
        grad = lax.all_gather(block, "tensor", axis=0, tiled=False)
        return jnp.transpose(grad, (1, 0, 2, 3)).reshape(2, -1, rows)

    def spread(value, mask):
        if not ring:
            total = lax.psum(value.astype(jnp.float32), "tensor")
            return [swap(total, "dp", n_dp, mask) if mask else total]
        got = [value] if not mask else []
        for step in range(0 if mask else 1, n_tensor):
            pairs = [
                (z * n_dp + d, (z + step) % n_tensor * n_dp + (d ^ mask))
                for z in range(n_tensor)
                for d in range(n_dp)
            ]
            got.append(lax.ppermute(value, ("tensor", "dp"), pairs))
        return got

    weights = (down_weight, swap(down_weight, "dp", n_dp, near))

    cut = lambda source, offset, span: source[:, offset : offset + span]
    start_gate = cut(gate_pre, offsets[-1], spans[-1]) if spans else None
    own_blocks = split_blocks(out_grad, 0, (start_gate,) if spans else ())
    far_blocks = split_blocks(out_grad, n_dp // 2, (own_blocks,))
    if spans:
        start_gate = swap(start_gate, "dp", n_dp, far)
    far_query = swap(queries, "dp", n_dp, far)
    far_blocks, start_gate, _ = lax.optimization_barrier((far_blocks, start_gate, far_query))
    far_start = swap(far_blocks, "dp", n_dp, far)
    own = [own_blocks, onward(own_blocks)] if ring and n_tensor > 1 else [own_blocks]
    later_gate, _ = lax.optimization_barrier((gate_pre, own_blocks))
    parts = [cut(later_gate, 0, main)]
    parts += [cut(later_gate, offset, span) for offset, span in zip(offsets[:-1], spans)]
    parts, _ = lax.optimization_barrier((parts, own[-1]))
    far_gate, *last_gates = [swap(part, "dp", n_dp, far) for part in parts]

    def all_pairs(hold):
        blocks, _ = lax.optimization_barrier(((queries, far_query), hold))
        blocks += tuple(swap(block, "dp", n_dp, near) for block in blocks)
        width = queries.shape[1]
        merged = jnp.zeros((queries.shape[0], n_dp * width), queries.dtype)
        for mask, block in zip((0, far, near, far ^ near), blocks):
            merged = lax.dynamic_update_slice(merged, block, (0, (me ^ mask) * width))
        return pair_queries(merged, proj_in.shape[1])

    proj_out = proj_out.T
    if ring and n_tensor > 1:
        split = n_tensor // 2
        while len(own) <= split:
            own.append(onward(own[-1]))
        own_early = list(enumerate(own))[:split]
        middle = -(-hidden // (2 * TILE)) * TILE if hidden % TILE == 0 else hidden
        halves = [(s, min(middle, hidden - s)) for s in range(0, hidden, middle)]
        own_sum, after = None, ()
        for s, span in halves:
            (own_sum,) = project(
                shard, own_early, gate_pre, weights, proj_out, s, span, 0, s, own_sum, None, after
            )
            if s == 0:
                first_sum = own_sum
            after = (own[-1],)
        early_sum = own_sum
        pairs = all_pairs(early_sum)
        others = [far_start]
        for _ in range(split - 1):
            others.append(onward(others[-1]))
        far_early = list(enumerate(others))
        (partial,) = project(
            shard, far_early, None, weights, proj_out, 0, 0, hidden, 0, None, None, (own_sum,)
        )
        while len(own) < n_tensor:
            own.append(onward(own[-1], first_sum))
        own_late = list(enumerate(own))[split:]
        after = (partial,)
        for s, span in halves:
            (own_sum,) = project(
                shard, own_late, gate_pre, weights, proj_out, s, span, 0, s, own_sum, None, after
            )
            if s == 0:
                while len(others) < n_tensor:
                    hold = own_sum if len(others) == n_tensor - 1 else early_sum
                    others.append(onward(others[-1], hold))
            after = (pairs, others[-2])
        far_late = list(enumerate(others))[split:]
    else:
        (own_sum,) = project(
            shard, [(0, gather(own_blocks))], gate_pre, weights, proj_out, 0, hidden, 0, 0, None, None, ()
        )
        far_late, partial = [(0, gather(far_start))], None
        pairs = all_pairs(own_sum)

    input_part = lax.dot_general(
        proj_in, inputs, (((0,), (1,)), ((), ())), preferred_element_type=jnp.float32
    )
    both = jnp.concatenate([input_part, own_sum])
    both, far_gate = lax.optimization_barrier((both, far_gate))
    terms = spread(both, 0)

    far_sum, *later = project(
        shard, far_late, far_gate, weights, proj_out, 0, main, sum(spans), 0, None, partial, (own_sum,)
    )
    if later:
        order = [len(spans) - 1] + list(range(len(spans) - 1))
        for k, gate in zip(order, [start_gate] + last_gates):
            final = k == order[-1]
            far_sum = finish(
                later[0],
                offsets[k] - main,
                gate,
                proj_out,
                offsets[k],
                far_sum,
                jnp.bfloat16 if final else jnp.float32,
                tuple(terms[1:]) if final else (),
            )
    return score(terms, spread(far_sum, far), pairs)


def solution(mesh):
    return jax.shard_map(
        functools.partial(on_device, mesh.shape["dp"], mesh.shape["tensor"]),
        mesh=mesh,
        in_specs=(
            P(("parts", "dp"), "tensor"),
            P(("parts", "dp"), None, "tensor"),
            P(("parts", "dp"), "tensor"),
            P("tensor", "dp"),
            P("tensor", None),
            P("tensor", None),
            P("tensor", "dp"),
        ),
        out_specs=P("tensor", ("parts", "dp")),
        check_vma=False,
    )
```

```python
import functools

import jax
import jax.numpy as jnp
from jax import lax
from jax.experimental import pallas as pl
from jax.experimental.pallas import tpu as pltpu
from jax.sharding import PartitionSpec as P

TILE = 1024
SMALL = 512
RING = 4
VMEM = 60 * 1024 * 1024
ANY = pl.BlockSpec(memory_space=pl.ANY)


def swap(value, axis, size, mask):
    return lax.ppermute(value, axis, [(i, i ^ mask) for i in range(size)])


def split_kernel(first, grad_ref, *refs):
    me = lax.axis_index("dp")
    out_ref = refs[-1]
    blocks = [grad_ref[:, k, :] for k in range(grad_ref.shape[1])]
    bit = 1
    while bit < len(blocks):
        flip = (me & bit) != 0
        blocks = [jnp.where(flip, blocks[k ^ bit], blocks[k]) for k in range(len(blocks))]
        bit *= 2
    for k in range(out_ref.shape[0]):
        out_ref[k] = blocks[first + k].T


def split_blocks(out_grad, first, after):
    rows, n, width = out_grad.shape
    step = rows // 4
    return pl.pallas_call(
        functools.partial(split_kernel, first),
        grid=(4,),
        in_specs=[pl.BlockSpec((step, n, width), lambda i: (i, 0, 0))] + [ANY] * len(after),
        out_specs=pl.BlockSpec((n // 2, width, step), lambda i: (0, 0, i)),
        out_shape=jax.ShapeDtypeStruct((n // 2, width, rows), out_grad.dtype),
        compiler_params=pltpu.CompilerParams(vmem_limit_bytes=VMEM),
        name="split_blocks",
    )(out_grad, *after)


def gated(hidden, gate_ref, proj_ref):
    gate = gate_ref[...].T.astype(jnp.float32)
    silu = gate * (0.5 + 0.5 * jnp.tanh(0.5 * gate))
    up_grad = (hidden * silu).astype(jnp.bfloat16)
    return jnp.dot(proj_ref[...], up_grad, preferred_element_type=jnp.float32)


def project_kernel(tiles, ahead, pieces, chained, carried, shard_ref, *refs):
    refs = list(refs)
    take = lambda n: [refs.pop(0) for _ in range(n)]
    grads = take(pieces)
    weights = take(2 * pieces)
    gate_ref, proj_ref = take(2) if tiles else (None, None)
    (before_ref,) = take(1) if chained else (None,)
    (partial_ref,) = take(1) if carried else (None,)
    sum_ref, odd_ref, even_ref = [refs.pop() for _ in range(3)] if tiles else (None,) * 3
    later_ref = refs.pop() if ahead else None
    out_ref = refs.pop() if tiles else None
    step = pl.program_id(0)

    def multiply(hidden_ref):
        hidden = partial_ref[...] if carried else None
        for k, grad_ref in enumerate(grads):
            for p in range(2):
                term = jnp.dot(
                    weights[2 * k + p][...], grad_ref[p], preferred_element_type=jnp.float32
                )
                hidden = term if hidden is None else hidden + term
        hidden_ref[...] = hidden

    if not tiles:
        multiply(later_ref)
        return

    def reduce(hidden_ref):
        sum_ref[...] += gated(hidden_ref[...], gate_ref, proj_ref)

    @pl.when(step == 0)
    def _():
        sum_ref[...] = before_ref[...] if chained else jnp.zeros_like(sum_ref)
        odd_ref[...] = jnp.zeros_like(odd_ref)

    @pl.when((step < tiles) & (lax.rem(step, 2) == 0))
    def _():
        reduce(odd_ref)
        multiply(even_ref)

    if tiles > 1:

        @pl.when((step < tiles) & (lax.rem(step, 2) == 1))
        def _():
            reduce(even_ref)
            multiply(odd_ref)

    @pl.when(step == tiles)
    def _():
        reduce(even_ref if tiles % 2 else odd_ref)
        out_ref[...] = sum_ref[...]

    if ahead:

        @pl.when(step >= tiles)
        def _():
            multiply(later_ref)


def project(shard, grads, gate, weights, proj, offset, span, extra, gate_column, before, partial, after):
    places = [place for place, _ in grads]
    pieces = [piece for _, piece in grads]
    _, width, rows = pieces[0].shape
    count = weights[0].shape[1] // width
    k = proj.shape[0]
    tile = TILE if (span + extra) % TILE == 0 else span + extra
    tiles, ahead = span // tile, extra // tile
    first, gate_first = offset // tile, gate_column // tile
    now = lambda i: jnp.minimum(i, tiles + ahead - 1)
    last = lambda i: jnp.clip(i - 1, 0, max(tiles - 1, 0))
    chained, carried = before is not None, partial is not None
    total = pl.BlockSpec((k, rows), lambda i, s: (0, 0))
    later = pl.BlockSpec((tile, rows), lambda i, s: (jnp.maximum(i - tiles, 0), 0))

    def weight_spec(place):
        return pl.BlockSpec(
            (tile, width), lambda i, s: (first + now(i), lax.rem(s[0] + count - place, count))
        )

    specs = [pl.BlockSpec((2, width, rows), lambda i, s: (0, 0, 0)) for _ in pieces]
    specs += [weight_spec(place) for place in places for _ in range(2)]
    operands = pieces + [weight for _ in places for weight in weights]
    if tiles:
        specs += [
            pl.BlockSpec((rows, tile), lambda i, s: (0, gate_first + last(i))),
            pl.BlockSpec((k, tile), lambda i, s: (0, first + last(i))),
        ]
        operands += [gate, proj]
    if chained:
        specs.append(total)
        operands.append(before)
    if carried:
        specs.append(pl.BlockSpec((tile, rows), lambda i, s: (first + now(i), 0)))
        operands.append(partial)
    hidden = pltpu.VMEM((tile, rows), jnp.float32)
    depth = 2 * width * len(pieces)
    return pl.pallas_call(
        functools.partial(project_kernel, tiles, ahead, len(pieces), chained, carried),
        grid_spec=pltpu.PrefetchScalarGridSpec(
            num_scalar_prefetch=1,
            grid=(tiles + max(ahead, 1) if tiles else ahead,),
            in_specs=specs + [ANY] * len(after),
            out_specs=[total] * bool(tiles) + [later] * bool(ahead),
            scratch_shapes=[hidden, hidden, pltpu.VMEM((k, rows), jnp.float32)] if tiles else [],
        ),
        out_shape=[jax.ShapeDtypeStruct((k, rows), jnp.float32)] * bool(tiles)
        + [jax.ShapeDtypeStruct((extra, rows), jnp.float32)] * bool(ahead),
        compiler_params=pltpu.CompilerParams(vmem_limit_bytes=VMEM),
        cost_estimate=pl.CostEstimate(
            flops=2 * rows * (span + extra) * depth,
            bytes_accessed=2 * (span + extra) * (depth + rows),
            transcendentals=rows * span,
        ),
        name="project",
    )(shard, *operands, *after)


def finish_kernel(hidden_ref, gate_ref, proj_ref, before_ref, *refs):
    out_ref, sum_ref = refs[-2:]
    part = gated(hidden_ref[...], gate_ref, proj_ref)

    @pl.when(pl.program_id(0) == 0)
    def _():
        sum_ref[...] = before_ref[...] + part

    @pl.when(pl.program_id(0) > 0)
    def _():
        sum_ref[...] += part

    @pl.when(pl.program_id(0) == pl.num_programs(0) - 1)
    def _():
        out_ref[...] = sum_ref[...].astype(out_ref.dtype)


def finish(hidden, row, gate, proj, offset, before, dtype, after):
    rows, span = gate.shape
    k = proj.shape[0]
    start, first = row // SMALL, offset // SMALL
    total = pl.BlockSpec((k, rows), lambda i: (0, 0))
    return pl.pallas_call(
        finish_kernel,
        grid=(span // SMALL,),
        in_specs=[
            pl.BlockSpec((SMALL, rows), lambda i: (start + i, 0)),
            pl.BlockSpec((rows, SMALL), lambda i: (0, i)),
            pl.BlockSpec((k, SMALL), lambda i: (0, first + i)),
            total,
        ]
        + [ANY] * len(after),
        out_specs=total,
        out_shape=jax.ShapeDtypeStruct((k, rows), dtype),
        scratch_shapes=[pltpu.VMEM((k, rows), jnp.float32)],
        compiler_params=pltpu.CompilerParams(vmem_limit_bytes=VMEM),
        name="finish",
    )(hidden, gate, proj, before, *after)


def score_kernel(n_both, *refs):
    *parts, query_ref, out_ref = refs
    both = functools.reduce(jnp.add, [ref[...] for ref in parts[:n_both]])
    inputs, grad = jnp.split(both, 2)
    for part_ref in parts[n_both:]:
        grad += part_ref[...].astype(jnp.float32)
    high = grad.astype(jnp.bfloat16)
    low = (grad - high.astype(jnp.float32)).astype(jnp.bfloat16)
    both = jnp.concatenate([high, low], axis=0)
    count = out_ref.shape[0]
    k = inputs.shape[0]
    group = 8
    scores = jnp.zeros(out_ref.shape, jnp.float32)
    for i in range(0, k, group):
        part = jnp.dot(
            query_ref[i * count : (i + group) * count, :], both, preferred_element_type=jnp.float32
        )
        for n in range(group):
            scores += inputs[i + n : i + n + 1, :] * part[n * count : (n + 1) * count, :]
    out_ref[...] = scores


def pair_kernel(k, masks, *refs):
    *block_refs, out_ref = refs
    me = lax.axis_index("dp")
    count, width = block_refs[0].shape
    for mask, block_ref in zip(masks, block_refs):
        base = pl.multiple_of((me ^ mask) * (width // k * count), count)
        for i in range(width // k):
            part = block_ref[:, i * k : (i + 1) * k]
            out_ref[pl.ds(base + i * count, count), :] = jnp.concatenate([part, part], axis=1)


def pair_queries(blocks, masks, k):
    count, width = blocks[0].shape
    return pl.pallas_call(
        functools.partial(pair_kernel, k, masks),
        out_shape=jax.ShapeDtypeStruct((len(blocks) * width // k * count, 2 * k), blocks[0].dtype),
        compiler_params=pltpu.CompilerParams(vmem_limit_bytes=VMEM),
        name="pair_queries",
    )(*blocks)


def score(both, grads, pairs):
    k, rows = grads[0].shape
    return pl.pallas_call(
        functools.partial(score_kernel, len(both)),
        out_shape=jax.ShapeDtypeStruct((pairs.shape[0] // k, rows), jnp.float32),
        compiler_params=pltpu.CompilerParams(vmem_limit_bytes=VMEM),
        name="score",
    )(*both, *grads, pairs)


def chunks_of(hidden):
    units = hidden // TILE
    if hidden % TILE or units < 5:
        return hidden, []
    return hidden - 3 * TILE, [2 * TILE - SMALL, SMALL, TILE]


def on_device(n_dp, n_tensor, inputs, out_grad, gate_pre, down_weight, proj_in, proj_out, queries):
    rows = out_grad.shape[0]
    hidden = gate_pre.shape[1]
    me = lax.axis_index("dp")
    shard = lax.axis_index("tensor").astype(jnp.int32).reshape(1)
    far, near = n_dp // 2, 1
    ring = n_tensor <= RING
    main, spans = chunks_of(hidden)
    offsets = [main + sum(spans[:k]) for k in range(len(spans))]

    def onward(piece, hold=None):
        if hold is not None:
            piece, _ = lax.optimization_barrier((piece, hold))
        return lax.ppermute(piece, "tensor", [(i, (i + 1) % n_tensor) for i in range(n_tensor)])

    def gather(block):
        grad = lax.all_gather(block, "tensor", axis=0, tiled=False)
        return jnp.transpose(grad, (1, 0, 2, 3)).reshape(2, -1, rows)

    def spread(value, mask):
        if not ring:
            total = lax.psum(value.astype(jnp.float32), "tensor")
            return [swap(total, "dp", n_dp, mask) if mask else total]
        got = [value] if not mask else []
        for step in range(0 if mask else 1, n_tensor):
            pairs = [
                (z * n_dp + d, (z + step) % n_tensor * n_dp + (d ^ mask))
                for z in range(n_tensor)
                for d in range(n_dp)
            ]
            got.append(lax.ppermute(value, ("tensor", "dp"), pairs))
        return got

    weights = (down_weight, swap(down_weight, "dp", n_dp, near))

    cut = lambda source, offset, span: source[:, offset : offset + span]
    start_gate = cut(gate_pre, offsets[-1], spans[-1]) if spans else None
    own_blocks = split_blocks(out_grad, 0, (start_gate,) if spans else ())
    far_blocks = split_blocks(out_grad, n_dp // 2, (own_blocks,))
    if spans:
        start_gate = swap(start_gate, "dp", n_dp, far)
    far_query = swap(queries, "dp", n_dp, far)
    later_gate, _ = lax.optimization_barrier((gate_pre, own_blocks))
    parts = [cut(later_gate, 0, main)]
    parts += [cut(later_gate, offset, span) for offset, span in zip(offsets[:-1], spans)]
    far_blocks, start_gate, parts, _ = lax.optimization_barrier(
        (far_blocks, start_gate, parts, far_query)
    )
    far_start = swap(far_blocks, "dp", n_dp, far)
    own = [own_blocks, onward(own_blocks)] if ring and n_tensor > 1 else [own_blocks]
    parts, _ = lax.optimization_barrier((parts, own[-1]))
    far_gate, *last_gates = [swap(part, "dp", n_dp, far) for part in parts]

    def all_pairs(hold):
        blocks, _ = lax.optimization_barrier(((queries, far_query), hold))
        blocks += tuple(swap(block, "dp", n_dp, near) for block in blocks)
        return pair_queries(blocks, (0, far, near, far ^ near), proj_in.shape[1])

    proj_out = proj_out.T
    if ring and n_tensor > 1:
        split = n_tensor // 2
        while len(own) <= split:
            own.append(onward(own[-1]))
        own_early = list(enumerate(own))[:split]
        middle = hidden // (2 * TILE) * TILE if hidden % TILE == 0 else 0
        halves = [(s, n) for s, n in ((0, middle), (middle, hidden - middle)) if n]
        own_sum, after = None, ()
        for s, span in halves:
            (own_sum,) = project(
                shard, own_early, gate_pre, weights, proj_out, s, span, 0, s, own_sum, None, after
            )
            if s == 0:
                first_sum = own_sum
            after = (own[-1],)
        early_sum = own_sum
        pairs = all_pairs(early_sum)
        others = [far_start]
        for _ in range(split - 1):
            others.append(onward(others[-1], first_sum))
        far_early = list(enumerate(others))
        (partial,) = project(
            shard, far_early, None, weights, proj_out, 0, 0, hidden, 0, None, None, (own_sum,)
        )
        while len(own) < n_tensor:
            own.append(onward(own[-1], first_sum))
        own_late = list(enumerate(own))[split:]
        after = (partial,)
        for s, span in halves:
            (own_sum,) = project(
                shard, own_late, gate_pre, weights, proj_out, s, span, 0, s, own_sum, None, after
            )
            if s == 0:
                while len(others) < n_tensor:
                    hold = own_sum if len(others) == n_tensor - 1 else early_sum
                    others.append(onward(others[-1], hold))
            after = (pairs, others[-2])
        far_late = list(enumerate(others))[split:]
    else:
        (own_sum,) = project(
            shard, [(0, gather(own_blocks))], gate_pre, weights, proj_out, 0, hidden, 0, 0, None, None, ()
        )
        far_late, partial = [(0, gather(far_start))], None
        pairs = all_pairs(own_sum)

    input_part = lax.dot_general(
        proj_in, inputs, (((0,), (1,)), ((), ())), preferred_element_type=jnp.float32
    )
    both = jnp.concatenate([input_part, own_sum])
    both, far_gate = lax.optimization_barrier((both, far_gate))
    terms = spread(both, 0)

    far_sum, *later = project(
        shard, far_late, far_gate, weights, proj_out, 0, main, sum(spans), 0, None, partial, (own_sum,)
    )
    if later:
        order = [len(spans) - 1] + list(range(len(spans) - 1))
        for k, gate in zip(order, [start_gate] + last_gates):
            final = k == order[-1]
            far_sum = finish(
                later[0],
                offsets[k] - main,
                gate,
                proj_out,
                offsets[k],
                far_sum,
                jnp.bfloat16 if final else jnp.float32,
                tuple(terms[1:]) if final else (),
            )
    return score(terms, spread(far_sum, far), pairs)


def solution(mesh):
    return jax.shard_map(
        functools.partial(on_device, mesh.shape["dp"], mesh.shape["tensor"]),
        mesh=mesh,
        in_specs=(
            P(("parts", "dp"), "tensor"),
            P(("parts", "dp"), None, "tensor"),
            P(("parts", "dp"), "tensor"),
            P("tensor", "dp"),
            P("tensor", None),
            P("tensor", None),
            P("tensor", "dp"),
        ),
        out_specs=P("tensor", ("parts", "dp")),
        check_vma=False,
    )
```

```python
import functools

import jax
import jax.numpy as jnp
from jax import lax
from jax.experimental import pallas as pl
from jax.experimental.pallas import tpu as pltpu
from jax.sharding import PartitionSpec as P

TILE = 1024
SMALL = 512
RING = 4
VMEM = 60 * 1024 * 1024
ANY = pl.BlockSpec(memory_space=pl.ANY)


def swap(value, axis, size, mask):
    return lax.ppermute(value, axis, [(i, i ^ mask) for i in range(size)])


def split_kernel(first, grad_ref, *refs):
    me = lax.axis_index("dp")
    out_ref = refs[-1]
    blocks = [grad_ref[:, k, :] for k in range(grad_ref.shape[1])]
    bit = 1
    while bit < len(blocks):
        flip = (me & bit) != 0
        blocks = [jnp.where(flip, blocks[k ^ bit], blocks[k]) for k in range(len(blocks))]
        bit *= 2
    for k in range(out_ref.shape[0]):
        out_ref[k] = blocks[first + k].T


def split_blocks(out_grad, first, after):
    rows, n, width = out_grad.shape
    step = rows // 4
    return pl.pallas_call(
        functools.partial(split_kernel, first),
        grid=(4,),
        in_specs=[pl.BlockSpec((step, n, width), lambda i: (i, 0, 0))] + [ANY] * len(after),
        out_specs=pl.BlockSpec((n // 2, width, step), lambda i: (0, 0, i)),
        out_shape=jax.ShapeDtypeStruct((n // 2, width, rows), out_grad.dtype),
        compiler_params=pltpu.CompilerParams(vmem_limit_bytes=VMEM),
        name="split_blocks",
    )(out_grad, *after)


def gated(hidden, gate_ref, proj_ref):
    gate = gate_ref[...].T.astype(jnp.float32)
    silu = gate * (0.5 + 0.5 * jnp.tanh(0.5 * gate))
    up_grad = (hidden * silu).astype(jnp.bfloat16)
    return jnp.dot(proj_ref[...], up_grad, preferred_element_type=jnp.float32)


def project_kernel(tiles, ahead, pieces, chained, carried, shard_ref, *refs):
    refs = list(refs)
    take = lambda n: [refs.pop(0) for _ in range(n)]
    grads = take(pieces)
    weights = take(2 * pieces)
    gate_ref, proj_ref = take(2) if tiles else (None, None)
    (before_ref,) = take(1) if chained else (None,)
    (partial_ref,) = take(1) if carried else (None,)
    sum_ref = refs.pop() if tiles else None
    odd_ref, even_ref = [refs.pop() for _ in range(2)] if tiles and ahead else (None, None)
    later_ref = refs.pop() if ahead else None
    out_ref = refs.pop() if tiles else None
    step = pl.program_id(0)

    def product():
        hidden = partial_ref[...] if carried else None
        for k, grad_ref in enumerate(grads):
            for p in range(2):
                term = jnp.dot(
                    weights[2 * k + p][...], grad_ref[p], preferred_element_type=jnp.float32
                )
                hidden = term if hidden is None else hidden + term
        return hidden

    def multiply(hidden_ref):
        hidden_ref[...] = product()

    if not tiles:
        multiply(later_ref)
        return

    def reduce(hidden_ref):
        sum_ref[...] += gated(hidden_ref[...], gate_ref, proj_ref)

    @pl.when(step == 0)
    def _():
        sum_ref[...] = before_ref[...] if chained else jnp.zeros_like(sum_ref)

    if not ahead:
        sum_ref[...] += gated(product(), gate_ref, proj_ref)

        @pl.when(step == tiles - 1)
        def _():
            out_ref[...] = sum_ref[...]

        return

    @pl.when(step == 0)
    def _():
        odd_ref[...] = jnp.zeros_like(odd_ref)

    @pl.when((step < tiles) & (lax.rem(step, 2) == 0))
    def _():
        reduce(odd_ref)
        multiply(even_ref)

    if tiles > 1:

        @pl.when((step < tiles) & (lax.rem(step, 2) == 1))
        def _():
            reduce(even_ref)
            multiply(odd_ref)

    @pl.when(step == tiles)
    def _():
        reduce(even_ref if tiles % 2 else odd_ref)
        out_ref[...] = sum_ref[...]

    @pl.when(step >= tiles)
    def _():
        multiply(later_ref)


def project(shard, grads, gate, weights, proj, offset, span, extra, gate_column, before, partial, after):
    places = [place for place, _ in grads]
    pieces = [piece for _, piece in grads]
    _, width, rows = pieces[0].shape
    count = weights[0].shape[1] // width
    k = proj.shape[0]
    tile = TILE if (span + extra) % TILE == 0 else span + extra
    tiles, ahead = span // tile, extra // tile
    first, gate_first = offset // tile, gate_column // tile
    now = lambda i: jnp.minimum(i, tiles + ahead - 1)
    last = lambda i: jnp.clip(i - 1, 0, tiles - 1) if ahead else i
    chained, carried = before is not None, partial is not None
    total = pl.BlockSpec((k, rows), lambda i, s: (0, 0))
    later = pl.BlockSpec((tile, rows), lambda i, s: (jnp.maximum(i - tiles, 0), 0))

    def weight_spec(place):
        return pl.BlockSpec(
            (tile, width), lambda i, s: (first + now(i), lax.rem(s[0] + count - place, count))
        )

    specs = [pl.BlockSpec((2, width, rows), lambda i, s: (0, 0, 0)) for _ in pieces]
    specs += [weight_spec(place) for place in places for _ in range(2)]
    operands = pieces + [weight for _ in places for weight in weights]
    if tiles:
        specs += [
            pl.BlockSpec((rows, tile), lambda i, s: (0, gate_first + last(i))),
            pl.BlockSpec((k, tile), lambda i, s: (0, first + last(i))),
        ]
        operands += [gate, proj]
    if chained:
        specs.append(total)
        operands.append(before)
    if carried:
        specs.append(pl.BlockSpec((tile, rows), lambda i, s: (first + now(i), 0)))
        operands.append(partial)
    hidden = pltpu.VMEM((tile, rows), jnp.float32)
    depth = 2 * width * len(pieces)
    return pl.pallas_call(
        functools.partial(project_kernel, tiles, ahead, len(pieces), chained, carried),
        grid_spec=pltpu.PrefetchScalarGridSpec(
            num_scalar_prefetch=1,
            grid=(tiles + ahead,),
            in_specs=specs + [ANY] * len(after),
            out_specs=[total] * bool(tiles) + [later] * bool(ahead),
            scratch_shapes=[hidden, hidden] * bool(tiles and ahead)
            + [pltpu.VMEM((k, rows), jnp.float32)] * bool(tiles),
        ),
        out_shape=[jax.ShapeDtypeStruct((k, rows), jnp.float32)] * bool(tiles)
        + [jax.ShapeDtypeStruct((extra, rows), jnp.float32)] * bool(ahead),
        compiler_params=pltpu.CompilerParams(vmem_limit_bytes=VMEM),
        cost_estimate=pl.CostEstimate(
            flops=2 * rows * (span + extra) * depth,
            bytes_accessed=2 * (span + extra) * (depth + rows),
            transcendentals=rows * span,
        ),
        name="project",
    )(shard, *operands, *after)


def finish_kernel(hidden_ref, gate_ref, proj_ref, before_ref, *refs):
    out_ref, sum_ref = refs[-2:]
    part = gated(hidden_ref[...], gate_ref, proj_ref)

    @pl.when(pl.program_id(0) == 0)
    def _():
        sum_ref[...] = before_ref[...] + part

    @pl.when(pl.program_id(0) > 0)
    def _():
        sum_ref[...] += part

    @pl.when(pl.program_id(0) == pl.num_programs(0) - 1)
    def _():
        out_ref[...] = sum_ref[...].astype(out_ref.dtype)


def finish(hidden, row, gate, proj, offset, before, dtype, after):
    rows, span = gate.shape
    k = proj.shape[0]
    start, first = row // SMALL, offset // SMALL
    total = pl.BlockSpec((k, rows), lambda i: (0, 0))
    return pl.pallas_call(
        finish_kernel,
        grid=(span // SMALL,),
        in_specs=[
            pl.BlockSpec((SMALL, rows), lambda i: (start + i, 0)),
            pl.BlockSpec((rows, SMALL), lambda i: (0, i)),
            pl.BlockSpec((k, SMALL), lambda i: (0, first + i)),
            total,
        ]
        + [ANY] * len(after),
        out_specs=total,
        out_shape=jax.ShapeDtypeStruct((k, rows), dtype),
        scratch_shapes=[pltpu.VMEM((k, rows), jnp.float32)],
        compiler_params=pltpu.CompilerParams(vmem_limit_bytes=VMEM),
        name="finish",
    )(hidden, gate, proj, before, *after)


def score_kernel(n_both, *refs):
    *parts, query_ref, out_ref = refs
    both = functools.reduce(jnp.add, [ref[...] for ref in parts[:n_both]])
    inputs, grad = jnp.split(both, 2)
    for part_ref in parts[n_both:]:
        grad += part_ref[...].astype(jnp.float32)
    high = grad.astype(jnp.bfloat16)
    low = (grad - high.astype(jnp.float32)).astype(jnp.bfloat16)
    both = jnp.concatenate([high, low], axis=0)
    count = out_ref.shape[0]
    k = inputs.shape[0]
    group = 8
    scores = jnp.zeros(out_ref.shape, jnp.float32)
    for i in range(0, k, group):
        part = jnp.dot(
            query_ref[i * count : (i + group) * count, :], both, preferred_element_type=jnp.float32
        )
        for n in range(group):
            scores += inputs[i + n : i + n + 1, :] * part[n * count : (n + 1) * count, :]
    out_ref[...] = scores


def pair_kernel(k, masks, *refs):
    *block_refs, out_ref = refs
    me = lax.axis_index("dp")
    count, width = block_refs[0].shape
    for mask, block_ref in zip(masks, block_refs):
        base = pl.multiple_of((me ^ mask) * (width // k * count), count)
        for i in range(width // k):
            part = block_ref[:, i * k : (i + 1) * k]
            out_ref[pl.ds(base + i * count, count), :] = jnp.concatenate([part, part], axis=1)


def pair_queries(blocks, masks, k):
    count, width = blocks[0].shape
    return pl.pallas_call(
        functools.partial(pair_kernel, k, masks),
        out_shape=jax.ShapeDtypeStruct((len(blocks) * width // k * count, 2 * k), blocks[0].dtype),
        compiler_params=pltpu.CompilerParams(vmem_limit_bytes=VMEM),
        name="pair_queries",
    )(*blocks)


def score(both, grads, pairs):
    k, rows = grads[0].shape
    return pl.pallas_call(
        functools.partial(score_kernel, len(both)),
        out_shape=jax.ShapeDtypeStruct((pairs.shape[0] // k, rows), jnp.float32),
        compiler_params=pltpu.CompilerParams(vmem_limit_bytes=VMEM),
        name="score",
    )(*both, *grads, pairs)


def chunks_of(hidden):
    units = hidden // TILE
    if hidden % TILE or units < 5:
        return hidden, []
    return hidden - 3 * TILE, [2 * TILE - SMALL, SMALL, TILE]


def on_device(n_dp, n_tensor, inputs, out_grad, gate_pre, down_weight, proj_in, proj_out, queries):
    rows = out_grad.shape[0]
    hidden = gate_pre.shape[1]
    me = lax.axis_index("dp")
    shard = lax.axis_index("tensor").astype(jnp.int32).reshape(1)
    far, near = n_dp // 2, 1
    ring = n_tensor <= RING
    main, spans = chunks_of(hidden)
    offsets = [main + sum(spans[:k]) for k in range(len(spans))]

    def onward(piece, hold=None):
        if hold is not None:
            piece, _ = lax.optimization_barrier((piece, hold))
        return lax.ppermute(piece, "tensor", [(i, (i + 1) % n_tensor) for i in range(n_tensor)])

    def gather(block):
        grad = lax.all_gather(block, "tensor", axis=0, tiled=False)
        return jnp.transpose(grad, (1, 0, 2, 3)).reshape(2, -1, rows)

    def spread(value, mask):
        if not ring:
            total = lax.psum(value.astype(jnp.float32), "tensor")
            return [swap(total, "dp", n_dp, mask) if mask else total]
        got = [value] if not mask else []
        for step in range(0 if mask else 1, n_tensor):
            pairs = [
                (z * n_dp + d, (z + step) % n_tensor * n_dp + (d ^ mask))
                for z in range(n_tensor)
                for d in range(n_dp)
            ]
            got.append(lax.ppermute(value, ("tensor", "dp"), pairs))
        return got

    weights = (down_weight, swap(down_weight, "dp", n_dp, near))

    cut = lambda source, offset, span: source[:, offset : offset + span]
    start_gate = cut(gate_pre, offsets[-1], spans[-1]) if spans else None
    own_blocks = split_blocks(out_grad, 0, (start_gate,) if spans else ())
    far_blocks = split_blocks(out_grad, n_dp // 2, (own_blocks,))
    if spans:
        start_gate = swap(start_gate, "dp", n_dp, far)
    far_query = swap(queries, "dp", n_dp, far)
    later_gate, _ = lax.optimization_barrier((gate_pre, own_blocks))
    parts = [cut(later_gate, 0, main)]
    parts += [cut(later_gate, offset, span) for offset, span in zip(offsets[:-1], spans)]
    far_blocks, start_gate, parts, _ = lax.optimization_barrier(
        (far_blocks, start_gate, parts, far_query)
    )
    far_start = swap(far_blocks, "dp", n_dp, far)
    own = [own_blocks, onward(own_blocks)] if ring and n_tensor > 1 else [own_blocks]
    parts, _ = lax.optimization_barrier((parts, own[-1]))
    far_gate, *last_gates = [swap(part, "dp", n_dp, far) for part in parts[: len(parts) - bool(spans)]]

    def all_pairs(hold):
        blocks, _ = lax.optimization_barrier(((queries, far_query), hold))
        blocks += tuple(swap(block, "dp", n_dp, near) for block in blocks)
        return pair_queries(blocks, (0, far, near, far ^ near), proj_in.shape[1])

    proj_out = proj_out.T
    if ring and n_tensor > 1:
        split = n_tensor // 2
        while len(own) <= split:
            own.append(onward(own[-1]))
        own_early = list(enumerate(own))[:split]
        units = hidden // TILE if hidden % TILE == 0 else 0
        halves = lambda cut: [(s, n) for s, n in ((0, cut * TILE), (cut * TILE, hidden - cut * TILE)) if n]
        own_sum, after = None, ()
        for s, span in halves(units // 3):
            (own_sum,) = project(
                shard, own_early, gate_pre, weights, proj_out, s, span, 0, s, own_sum, None, after
            )
            if s == 0:
                first_sum = own_sum
            after = (own[-1],)
        early_sum = own_sum
        pairs = all_pairs(early_sum)
        others = [far_start]
        for _ in range(split - 1):
            others.append(onward(others[-1], first_sum))
        far_early = list(enumerate(others))
        (partial,) = project(
            shard, far_early, None, weights, proj_out, 0, 0, hidden, 0, None, None, (own_sum,)
        )
        while len(own) < n_tensor:
            own.append(onward(own[-1], first_sum))
        own_late = list(enumerate(own))[split:]
        after = (partial, pairs)
        for s, span in halves(units // 2):
            (own_sum,) = project(
                shard, own_late, gate_pre, weights, proj_out, s, span, 0, s, own_sum, None, after
            )
            if s == 0:
                while len(others) < n_tensor:
                    hold = own_sum if len(others) == n_tensor - 1 else early_sum
                    others.append(onward(others[-1], hold))
            after = (others[-2],)
        far_late = list(enumerate(others))[split:]
    else:
        (own_sum,) = project(
            shard, [(0, gather(own_blocks))], gate_pre, weights, proj_out, 0, hidden, 0, 0, None, None, ()
        )
        far_late, partial = [(0, gather(far_start))], None
        pairs = all_pairs(own_sum)

    input_part = lax.dot_general(
        proj_in, inputs, (((0,), (1,)), ((), ())), preferred_element_type=jnp.float32
    )
    both = jnp.concatenate([input_part, own_sum])
    both, far_gate = lax.optimization_barrier((both, far_gate))
    terms = [lax.psum(both, "tensor")]

    if spans:
        final_gate, own_sum = lax.optimization_barrier((parts[-1], own_sum))
        last_gates.append(swap(final_gate, "dp", n_dp, far))
    far_sum, *later = project(
        shard, far_late, far_gate, weights, proj_out, 0, main, sum(spans), 0, None, partial, (own_sum,)
    )
    if later:
        order = [len(spans) - 1] + list(range(len(spans) - 1))
        for k, gate in zip(order, [start_gate] + last_gates):
            final = k == order[-1]
            far_sum = finish(
                later[0],
                offsets[k] - main,
                gate,
                proj_out,
                offsets[k],
                far_sum,
                jnp.bfloat16 if final else jnp.float32,
                (),
            )
    return score(terms, spread(far_sum, far), pairs)


def solution(mesh):
    return jax.shard_map(
        functools.partial(on_device, mesh.shape["dp"], mesh.shape["tensor"]),
        mesh=mesh,
        in_specs=(
            P(("parts", "dp"), "tensor"),
            P(("parts", "dp"), None, "tensor"),
            P(("parts", "dp"), "tensor"),
            P("tensor", "dp"),
            P("tensor", None),
            P("tensor", None),
            P("tensor", "dp"),
        ),
        out_specs=P("tensor", ("parts", "dp")),
        check_vma=False,
    )
```

```python
import functools

import jax
import jax.numpy as jnp
from jax import lax
from jax.experimental import pallas as pl
from jax.experimental.pallas import tpu as pltpu
from jax.sharding import PartitionSpec as P

TILE = 1024
SMALL = 512
RING = 4
VMEM = 60 * 1024 * 1024
ANY = pl.BlockSpec(memory_space=pl.ANY)


def swap(value, axis, size, mask):
    return lax.ppermute(value, axis, [(i, i ^ mask) for i in range(size)])


def split_kernel(first, grad_ref, *refs):
    me = lax.axis_index("dp")
    out_ref = refs[-1]
    blocks = [grad_ref[:, k, :] for k in range(grad_ref.shape[1])]
    bit = 1
    while bit < len(blocks):
        flip = (me & bit) != 0
        blocks = [jnp.where(flip, blocks[k ^ bit], blocks[k]) for k in range(len(blocks))]
        bit *= 2
    for k in range(out_ref.shape[0]):
        out_ref[k] = blocks[first + k].T


def split_blocks(out_grad, first, after):
    rows, n, width = out_grad.shape
    step = rows // 4
    return pl.pallas_call(
        functools.partial(split_kernel, first),
        grid=(4,),
        in_specs=[pl.BlockSpec((step, n, width), lambda i: (i, 0, 0))] + [ANY] * len(after),
        out_specs=pl.BlockSpec((n // 2, width, step), lambda i: (0, 0, i)),
        out_shape=jax.ShapeDtypeStruct((n // 2, width, rows), out_grad.dtype),
        compiler_params=pltpu.CompilerParams(vmem_limit_bytes=VMEM),
        name="split_blocks",
    )(out_grad, *after)


def gated(hidden, gate_ref, proj_ref):
    gate = gate_ref[...].T.astype(jnp.float32)
    silu = gate * (0.5 + 0.5 * jnp.tanh(0.5 * gate))
    up_grad = (hidden * silu).astype(jnp.bfloat16)
    return jnp.dot(proj_ref[...], up_grad, preferred_element_type=jnp.float32)


def project_kernel(tiles, ahead, pieces, chained, carried, shard_ref, *refs):
    refs = list(refs)
    take = lambda n: [refs.pop(0) for _ in range(n)]
    grads = take(pieces)
    weights = take(2 * pieces)
    gate_ref, proj_ref = take(2) if tiles else (None, None)
    (before_ref,) = take(1) if chained else (None,)
    (partial_ref,) = take(1) if carried else (None,)
    sum_ref = refs.pop() if tiles else None
    odd_ref, even_ref = [refs.pop() for _ in range(2)] if tiles and ahead else (None, None)
    later_ref = refs.pop() if ahead else None
    out_ref = refs.pop() if tiles else None
    step = pl.program_id(0)

    def product():
        hidden = partial_ref[...] if carried else None
        for k, grad_ref in enumerate(grads):
            for p in range(2):
                term = jnp.dot(
                    weights[2 * k + p][...], grad_ref[p], preferred_element_type=jnp.float32
                )
                hidden = term if hidden is None else hidden + term
        return hidden

    def multiply(hidden_ref):
        hidden_ref[...] = product()

    if not tiles:
        multiply(later_ref)
        return

    def reduce(hidden_ref):
        sum_ref[...] += gated(hidden_ref[...], gate_ref, proj_ref)

    @pl.when(step == 0)
    def _():
        sum_ref[...] = before_ref[...] if chained else jnp.zeros_like(sum_ref)

    if not ahead:
        sum_ref[...] += gated(product(), gate_ref, proj_ref)

        @pl.when(step == tiles - 1)
        def _():
            out_ref[...] = sum_ref[...]

        return

    @pl.when(step == 0)
    def _():
        odd_ref[...] = jnp.zeros_like(odd_ref)

    @pl.when((step < tiles) & (lax.rem(step, 2) == 0))
    def _():
        reduce(odd_ref)
        multiply(even_ref)

    if tiles > 1:

        @pl.when((step < tiles) & (lax.rem(step, 2) == 1))
        def _():
            reduce(even_ref)
            multiply(odd_ref)

    @pl.when(step == tiles)
    def _():
        reduce(even_ref if tiles % 2 else odd_ref)
        out_ref[...] = sum_ref[...]

    @pl.when(step >= tiles)
    def _():
        multiply(later_ref)


def project(shard, grads, gate, weights, proj, offset, span, extra, gate_column, before, partial, after):
    places = [place for place, _ in grads]
    pieces = [piece for _, piece in grads]
    _, width, rows = pieces[0].shape
    count = weights[0].shape[1] // width
    k = proj.shape[0]
    tile = TILE if (span + extra) % TILE == 0 else span + extra
    tiles, ahead = span // tile, extra // tile
    first, gate_first = offset // tile, gate_column // tile
    now = lambda i: jnp.minimum(i, tiles + ahead - 1)
    last = lambda i: jnp.clip(i - 1, 0, tiles - 1) if ahead else i
    chained, carried = before is not None, partial is not None
    total = pl.BlockSpec((k, rows), lambda i, s: (0, 0))
    later = pl.BlockSpec((tile, rows), lambda i, s: (jnp.maximum(i - tiles, 0), 0))

    def weight_spec(place):
        return pl.BlockSpec(
            (tile, width), lambda i, s: (first + now(i), lax.rem(s[0] + count - place, count))
        )

    specs = [pl.BlockSpec((2, width, rows), lambda i, s: (0, 0, 0)) for _ in pieces]
    specs += [weight_spec(place) for place in places for _ in range(2)]
    operands = pieces + [weight for _ in places for weight in weights]
    if tiles:
        specs += [
            pl.BlockSpec((rows, tile), lambda i, s: (0, gate_first + last(i))),
            pl.BlockSpec((k, tile), lambda i, s: (0, first + last(i))),
        ]
        operands += [gate, proj]
    if chained:
        specs.append(total)
        operands.append(before)
    if carried:
        specs.append(pl.BlockSpec((tile, rows), lambda i, s: (first + now(i), 0)))
        operands.append(partial)
    hidden = pltpu.VMEM((tile, rows), jnp.float32)
    depth = 2 * width * len(pieces)
    return pl.pallas_call(
        functools.partial(project_kernel, tiles, ahead, len(pieces), chained, carried),
        grid_spec=pltpu.PrefetchScalarGridSpec(
            num_scalar_prefetch=1,
            grid=(tiles + ahead,),
            in_specs=specs + [ANY] * len(after),
            out_specs=[total] * bool(tiles) + [later] * bool(ahead),
            scratch_shapes=[hidden, hidden] * bool(tiles and ahead)
            + [pltpu.VMEM((k, rows), jnp.float32)] * bool(tiles),
        ),
        out_shape=[jax.ShapeDtypeStruct((k, rows), jnp.float32)] * bool(tiles)
        + [jax.ShapeDtypeStruct((extra, rows), jnp.float32)] * bool(ahead),
        compiler_params=pltpu.CompilerParams(vmem_limit_bytes=VMEM),
        cost_estimate=pl.CostEstimate(
            flops=2 * rows * (span + extra) * depth,
            bytes_accessed=2 * (span + extra) * (depth + rows),
            transcendentals=rows * span,
        ),
        name="project",
    )(shard, *operands, *after)


def finish_kernel(hidden_ref, gate_ref, proj_ref, before_ref, *refs):
    out_ref, sum_ref = refs[-2:]
    part = gated(hidden_ref[...], gate_ref, proj_ref)

    @pl.when(pl.program_id(0) == 0)
    def _():
        sum_ref[...] = before_ref[...] + part

    @pl.when(pl.program_id(0) > 0)
    def _():
        sum_ref[...] += part

    @pl.when(pl.program_id(0) == pl.num_programs(0) - 1)
    def _():
        out_ref[...] = sum_ref[...].astype(out_ref.dtype)


def finish(hidden, row, gate, proj, offset, before, dtype, after):
    rows, span = gate.shape
    k = proj.shape[0]
    start, first = row // SMALL, offset // SMALL
    total = pl.BlockSpec((k, rows), lambda i: (0, 0))
    return pl.pallas_call(
        finish_kernel,
        grid=(span // SMALL,),
        in_specs=[
            pl.BlockSpec((SMALL, rows), lambda i: (start + i, 0)),
            pl.BlockSpec((rows, SMALL), lambda i: (0, i)),
            pl.BlockSpec((k, SMALL), lambda i: (0, first + i)),
            total,
        ]
        + [ANY] * len(after),
        out_specs=total,
        out_shape=jax.ShapeDtypeStruct((k, rows), dtype),
        scratch_shapes=[pltpu.VMEM((k, rows), jnp.float32)],
        compiler_params=pltpu.CompilerParams(vmem_limit_bytes=VMEM),
        name="finish",
    )(hidden, gate, proj, before, *after)


def score_kernel(n_both, *refs):
    *parts, query_ref, out_ref = refs
    both = functools.reduce(jnp.add, [ref[...] for ref in parts[:n_both]])
    inputs, grad = jnp.split(both, 2)
    for part_ref in parts[n_both:]:
        grad += part_ref[...].astype(jnp.float32)
    high = grad.astype(jnp.bfloat16)
    low = (grad - high.astype(jnp.float32)).astype(jnp.bfloat16)
    both = jnp.concatenate([high, low], axis=0)
    count = out_ref.shape[0]
    k = inputs.shape[0]
    group = 8
    scores = jnp.zeros(out_ref.shape, jnp.float32)
    for i in range(0, k, group):
        part = jnp.dot(
            query_ref[i * count : (i + group) * count, :], both, preferred_element_type=jnp.float32
        )
        for n in range(group):
            scores += inputs[i + n : i + n + 1, :] * part[n * count : (n + 1) * count, :]
    out_ref[...] = scores


def pair_kernel(k, masks, *refs):
    *block_refs, out_ref = refs
    me = lax.axis_index("dp")
    count, width = block_refs[0].shape
    for mask, block_ref in zip(masks, block_refs):
        base = pl.multiple_of((me ^ mask) * (width // k * count), count)
        for i in range(width // k):
            part = block_ref[:, i * k : (i + 1) * k]
            out_ref[pl.ds(base + i * count, count), :] = jnp.concatenate([part, part], axis=1)


def pair_queries(blocks, masks, k):
    count, width = blocks[0].shape
    return pl.pallas_call(
        functools.partial(pair_kernel, k, masks),
        out_shape=jax.ShapeDtypeStruct((len(blocks) * width // k * count, 2 * k), blocks[0].dtype),
        compiler_params=pltpu.CompilerParams(vmem_limit_bytes=VMEM),
        name="pair_queries",
    )(*blocks)


def score(both, grads, pairs):
    k, rows = grads[0].shape
    return pl.pallas_call(
        functools.partial(score_kernel, len(both)),
        out_shape=jax.ShapeDtypeStruct((pairs.shape[0] // k, rows), jnp.float32),
        compiler_params=pltpu.CompilerParams(vmem_limit_bytes=VMEM),
        name="score",
    )(*both, *grads, pairs)


def chunks_of(hidden):
    units = hidden // TILE
    if hidden % TILE or units < 5:
        return hidden, []
    return hidden - 3 * TILE, [2 * TILE - SMALL, SMALL, TILE]


def on_device(n_dp, n_tensor, inputs, out_grad, gate_pre, down_weight, proj_in, proj_out, queries):
    rows = out_grad.shape[0]
    hidden = gate_pre.shape[1]
    me = lax.axis_index("dp")
    shard = lax.axis_index("tensor").astype(jnp.int32).reshape(1)
    far, near = n_dp // 2, 1
    ring = n_tensor <= RING
    main, spans = chunks_of(hidden)
    offsets = [main + sum(spans[:k]) for k in range(len(spans))]

    def onward(piece, hold=None):
        if hold is not None:
            piece, _ = lax.optimization_barrier((piece, hold))
        return lax.ppermute(piece, "tensor", [(i, (i + 1) % n_tensor) for i in range(n_tensor)])

    def gather(block):
        grad = lax.all_gather(block, "tensor", axis=0, tiled=False)
        return jnp.transpose(grad, (1, 0, 2, 3)).reshape(2, -1, rows)

    def spread(value, mask):
        if not ring:
            total = lax.psum(value.astype(jnp.float32), "tensor")
            return [swap(total, "dp", n_dp, mask) if mask else total]
        got = [value] if not mask else []
        for step in range(0 if mask else 1, n_tensor):
            pairs = [
                (z * n_dp + d, (z + step) % n_tensor * n_dp + (d ^ mask))
                for z in range(n_tensor)
                for d in range(n_dp)
            ]
            got.append(lax.ppermute(value, ("tensor", "dp"), pairs))
        return got

    weights = (down_weight, swap(down_weight, "dp", n_dp, near))

    cut = lambda source, offset, span: source[:, offset : offset + span]
    start_gate = cut(gate_pre, offsets[-1], spans[-1]) if spans else None
    own_blocks = split_blocks(out_grad, 0, (start_gate,) if spans else ())
    far_blocks = split_blocks(out_grad, n_dp // 2, (own_blocks,))
    if spans:
        start_gate = swap(start_gate, "dp", n_dp, far)
    far_query = swap(queries, "dp", n_dp, far)
    later_gate, _ = lax.optimization_barrier((gate_pre, own_blocks))
    parts = [cut(later_gate, 0, main)]
    parts += [cut(later_gate, offset, span) for offset, span in zip(offsets[:-1], spans)]
    far_blocks, start_gate, parts, _ = lax.optimization_barrier(
        (far_blocks, start_gate, parts, far_query)
    )
    far_start = swap(far_blocks, "dp", n_dp, far)
    own = [own_blocks, onward(own_blocks)] if ring and n_tensor > 1 else [own_blocks]
    parts, _ = lax.optimization_barrier((parts, own[-1]))
    far_gate, *last_gates = [swap(part, "dp", n_dp, far) for part in parts[: len(parts) - bool(spans)]]

    def all_pairs(hold):
        blocks, _ = lax.optimization_barrier(((queries, far_query), hold))
        blocks += tuple(swap(block, "dp", n_dp, near) for block in blocks)
        return pair_queries(blocks, (0, far, near, far ^ near), proj_in.shape[1])

    proj_out = proj_out.T
    if ring and n_tensor > 1:
        split = n_tensor // 2
        while len(own) <= split:
            own.append(onward(own[-1]))
        own_early = list(enumerate(own))[:split]
        units = hidden // TILE if hidden % TILE == 0 else 0
        halves = lambda cut: [(s, n) for s, n in ((0, cut * TILE), (cut * TILE, hidden - cut * TILE)) if n]
        own_sum, after = None, ()
        for s, span in halves(units // 3):
            (own_sum,) = project(
                shard, own_early, gate_pre, weights, proj_out, s, span, 0, s, own_sum, None, after
            )
            if s == 0:
                first_sum = own_sum
            after = (own[-1],)
        early_sum = own_sum
        pairs = all_pairs(own[1])
        others = [far_start]
        for _ in range(split - 1):
            others.append(onward(others[-1], first_sum))
        far_early = list(enumerate(others))
        (partial,) = project(
            shard, far_early, None, weights, proj_out, 0, 0, hidden, 0, None, None, (own_sum,)
        )
        while len(own) < n_tensor:
            own.append(onward(own[-1], first_sum))
        own_late = list(enumerate(own))[split:]
        after = (partial, pairs)
        for s, span in halves(units // 2):
            (own_sum,) = project(
                shard, own_late, gate_pre, weights, proj_out, s, span, 0, s, own_sum, None, after
            )
            if s == 0:
                while len(others) < n_tensor:
                    hold = own_sum if len(others) == n_tensor - 1 else early_sum
                    others.append(onward(others[-1], hold))
            after = (others[-2],)
        far_late = list(enumerate(others))[split:]
    else:
        (own_sum,) = project(
            shard, [(0, gather(own_blocks))], gate_pre, weights, proj_out, 0, hidden, 0, 0, None, None, ()
        )
        far_late, partial = [(0, gather(far_start))], None
        pairs = all_pairs(own_sum)

    input_part = lax.dot_general(
        proj_in, inputs, (((0,), (1,)), ((), ())), preferred_element_type=jnp.float32
    )
    both = jnp.concatenate([input_part, own_sum])
    both, far_gate = lax.optimization_barrier((both, far_gate))
    terms = spread(both, 0)

    if spans:
        final_gate, own_sum = lax.optimization_barrier((parts[-1], own_sum))
        last_gates.append(swap(final_gate, "dp", n_dp, far))
    far_sum, *later = project(
        shard, far_late, far_gate, weights, proj_out, 0, main, sum(spans), 0, None, partial, (own_sum,)
    )
    if later:
        order = [len(spans) - 1] + list(range(len(spans) - 1))
        for k, gate in zip(order, [start_gate] + last_gates):
            final = k == order[-1]
            far_sum = finish(
                later[0],
                offsets[k] - main,
                gate,
                proj_out,
                offsets[k],
                far_sum,
                jnp.bfloat16 if final else jnp.float32,
                (),
            )
    return score(terms, spread(far_sum, far), pairs)


def solution(mesh):
    return jax.shard_map(
        functools.partial(on_device, mesh.shape["dp"], mesh.shape["tensor"]),
        mesh=mesh,
        in_specs=(
            P(("parts", "dp"), "tensor"),
            P(("parts", "dp"), None, "tensor"),
            P(("parts", "dp"), "tensor"),
            P("tensor", "dp"),
            P("tensor", None),
            P("tensor", None),
            P("tensor", "dp"),
        ),
        out_specs=P("tensor", ("parts", "dp")),
        check_vma=False,
    )
```

```python
import functools

import jax
import jax.numpy as jnp
from jax import lax
from jax.experimental import pallas as pl
from jax.experimental.pallas import tpu as pltpu
from jax.sharding import PartitionSpec as P

TILE = 1024
SMALL = 512
RING = 4
VMEM = 60 * 1024 * 1024
ANY = pl.BlockSpec(memory_space=pl.ANY)


def swap(value, axis, size, mask):
    return lax.ppermute(value, axis, [(i, i ^ mask) for i in range(size)])


def split_kernel(first, grad_ref, *refs):
    me = lax.axis_index("dp")
    out_ref = refs[-1]
    blocks = [grad_ref[:, k, :] for k in range(grad_ref.shape[1])]
    bit = 1
    while bit < len(blocks):
        flip = (me & bit) != 0
        blocks = [jnp.where(flip, blocks[k ^ bit], blocks[k]) for k in range(len(blocks))]
        bit *= 2
    for k in range(out_ref.shape[0]):
        out_ref[k] = blocks[first + k].T


def split_blocks(out_grad, first, after):
    rows, n, width = out_grad.shape
    step = rows // 4
    return pl.pallas_call(
        functools.partial(split_kernel, first),
        grid=(4,),
        in_specs=[pl.BlockSpec((step, n, width), lambda i: (i, 0, 0))] + [ANY] * len(after),
        out_specs=pl.BlockSpec((n // 2, width, step), lambda i: (0, 0, i)),
        out_shape=jax.ShapeDtypeStruct((n // 2, width, rows), out_grad.dtype),
        compiler_params=pltpu.CompilerParams(vmem_limit_bytes=VMEM),
        name="split_blocks",
    )(out_grad, *after)


def gated(hidden, gate_ref, proj_ref):
    gate = gate_ref[...].T.astype(jnp.float32)
    silu = gate * (0.5 + 0.5 * jnp.tanh(0.5 * gate))
    up_grad = (hidden * silu).astype(jnp.bfloat16)
    return jnp.dot(proj_ref[...], up_grad, preferred_element_type=jnp.float32)


def project_kernel(tiles, ahead, pieces, chained, carried, tailed, shard_ref, *refs):
    refs = list(refs)
    take = lambda n: [refs.pop(0) for _ in range(n)]
    grads = take(pieces)
    weights = take(2 * pieces)
    gate_ref, proj_ref = take(2) if tiles else (None, None)
    (before_ref,) = take(1) if chained else (None,)
    (partial_ref,) = take(1) if carried else (None,)
    (tail_ref,) = take(1) if tailed else (None,)
    sum_ref = refs.pop() if tiles else None
    later_ref = refs.pop() if ahead else None
    out_ref = refs.pop() if tiles else None
    step = pl.program_id(0)

    def product():
        hidden = partial_ref[...] if carried else None
        for k, grad_ref in enumerate(grads):
            for p in range(2):
                term = jnp.dot(
                    weights[2 * k + p][...], grad_ref[p], preferred_element_type=jnp.float32
                )
                hidden = term if hidden is None else hidden + term
        return hidden

    if not tiles:
        later_ref[...] = product()
        return

    @pl.when(step == 0)
    def _():
        sum_ref[...] = before_ref[...] if chained else jnp.zeros_like(sum_ref)

    @pl.when(step < tiles)
    def _():
        sum_ref[...] += gated(product(), gate_ref, proj_ref)

    if ahead:

        @pl.when((step >= tiles) & (step < tiles + ahead))
        def _():
            later_ref[...] = product()

    if tailed:

        @pl.when(step == tiles + ahead)
        def _():
            sum_ref[...] += gated(product(), tail_ref, proj_ref)

    @pl.when(step == tiles + ahead + tailed - 1)
    def _():
        out_ref[...] = sum_ref[...]


def project(shard, grads, gate, weights, proj, offset, span, extra, gate_column, before, partial, after, tail=None):
    places = [place for place, _ in grads]
    pieces = [piece for _, piece in grads]
    _, width, rows = pieces[0].shape
    count = weights[0].shape[1] // width
    k = proj.shape[0]
    tile = TILE if (span + extra) % TILE == 0 else span + extra
    tiles, ahead = span // tile, extra // tile
    first, gate_first = offset // tile, gate_column // tile
    tailed = int(tail is not None)
    now = lambda i: i
    last = lambda i: jnp.minimum(i, tiles - 1)
    ends = lambda i: jnp.where(i < tiles + ahead, jnp.minimum(i, tiles - 1), i)
    chained, carried = before is not None, partial is not None
    total = pl.BlockSpec((k, rows), lambda i, s: (0, 0))
    later = pl.BlockSpec((tile, rows), lambda i, s: (jnp.clip(i - tiles, 0, ahead - 1), 0))

    def weight_spec(place):
        return pl.BlockSpec(
            (tile, width), lambda i, s: (first + now(i), lax.rem(s[0] + count - place, count))
        )

    specs = [pl.BlockSpec((2, width, rows), lambda i, s: (0, 0, 0)) for _ in pieces]
    specs += [weight_spec(place) for place in places for _ in range(2)]
    operands = pieces + [weight for _ in places for weight in weights]
    if tiles:
        specs += [
            pl.BlockSpec((rows, tile), lambda i, s: (0, gate_first + last(i))),
            pl.BlockSpec((k, tile), lambda i, s: (0, first + ends(i))),
        ]
        operands += [gate, proj]
    if chained:
        specs.append(total)
        operands.append(before)
    if carried:
        specs.append(pl.BlockSpec((tile, rows), lambda i, s: (first + now(i), 0)))
        operands.append(partial)
    if tailed:
        specs.append(pl.BlockSpec((rows, tile), lambda i, s: (0, 0)))
        operands.append(tail)
    depth = 2 * width * len(pieces)
    return pl.pallas_call(
        functools.partial(project_kernel, tiles, ahead, len(pieces), chained, carried, tailed),
        grid_spec=pltpu.PrefetchScalarGridSpec(
            num_scalar_prefetch=1,
            grid=(tiles + ahead + tailed,),
            in_specs=specs + [ANY] * len(after),
            out_specs=[total] * bool(tiles) + [later] * bool(ahead),
            scratch_shapes=[pltpu.VMEM((k, rows), jnp.float32)] * bool(tiles),
        ),
        out_shape=[jax.ShapeDtypeStruct((k, rows), jnp.float32)] * bool(tiles)
        + [jax.ShapeDtypeStruct((extra, rows), jnp.float32)] * bool(ahead),
        compiler_params=pltpu.CompilerParams(vmem_limit_bytes=VMEM),
        cost_estimate=pl.CostEstimate(
            flops=2 * rows * (span + extra) * depth,
            bytes_accessed=2 * (span + extra) * (depth + rows),
            transcendentals=rows * span,
        ),
        name="project",
    )(shard, *operands, *after)


def finish_kernel(hidden_ref, gate_ref, proj_ref, before_ref, *refs):
    out_ref, sum_ref = refs[-2:]
    part = gated(hidden_ref[...], gate_ref, proj_ref)

    @pl.when(pl.program_id(0) == 0)
    def _():
        sum_ref[...] = before_ref[...] + part

    @pl.when(pl.program_id(0) > 0)
    def _():
        sum_ref[...] += part

    @pl.when(pl.program_id(0) == pl.num_programs(0) - 1)
    def _():
        out_ref[...] = sum_ref[...].astype(out_ref.dtype)


def finish(hidden, row, gate, proj, offset, before, dtype, after):
    rows, span = gate.shape
    k = proj.shape[0]
    start, first = row // SMALL, offset // SMALL
    total = pl.BlockSpec((k, rows), lambda i: (0, 0))
    return pl.pallas_call(
        finish_kernel,
        grid=(span // SMALL,),
        in_specs=[
            pl.BlockSpec((SMALL, rows), lambda i: (start + i, 0)),
            pl.BlockSpec((rows, SMALL), lambda i: (0, i)),
            pl.BlockSpec((k, SMALL), lambda i: (0, first + i)),
            total,
        ]
        + [ANY] * len(after),
        out_specs=total,
        out_shape=jax.ShapeDtypeStruct((k, rows), dtype),
        scratch_shapes=[pltpu.VMEM((k, rows), jnp.float32)],
        compiler_params=pltpu.CompilerParams(vmem_limit_bytes=VMEM),
        name="finish",
    )(hidden, gate, proj, before, *after)


def score_kernel(n_both, *refs):
    *parts, query_ref, out_ref = refs
    both = functools.reduce(jnp.add, [ref[...] for ref in parts[:n_both]])
    inputs, grad = jnp.split(both, 2)
    for part_ref in parts[n_both:]:
        grad += part_ref[...].astype(jnp.float32)
    high = grad.astype(jnp.bfloat16)
    low = (grad - high.astype(jnp.float32)).astype(jnp.bfloat16)
    both = jnp.concatenate([high, low], axis=0)
    count = out_ref.shape[0]
    k = inputs.shape[0]
    group = 8
    scores = jnp.zeros(out_ref.shape, jnp.float32)
    for i in range(0, k, group):
        part = jnp.dot(
            query_ref[i * count : (i + group) * count, :], both, preferred_element_type=jnp.float32
        )
        for n in range(group):
            scores += inputs[i + n : i + n + 1, :] * part[n * count : (n + 1) * count, :]
    out_ref[...] = scores


def pair_kernel(k, masks, *refs):
    *block_refs, out_ref = refs
    me = lax.axis_index("dp")
    count, width = block_refs[0].shape
    for mask, block_ref in zip(masks, block_refs):
        base = pl.multiple_of((me ^ mask) * (width // k * count), count)
        for i in range(width // k):
            part = block_ref[:, i * k : (i + 1) * k]
            out_ref[pl.ds(base + i * count, count), :] = jnp.concatenate([part, part], axis=1)


def pair_queries(blocks, masks, k):
    count, width = blocks[0].shape
    return pl.pallas_call(
        functools.partial(pair_kernel, k, masks),
        out_shape=jax.ShapeDtypeStruct((len(blocks) * width // k * count, 2 * k), blocks[0].dtype),
        compiler_params=pltpu.CompilerParams(vmem_limit_bytes=VMEM),
        name="pair_queries",
    )(*blocks)


def score(both, grads, pairs):
    k, rows = grads[0].shape
    return pl.pallas_call(
        functools.partial(score_kernel, len(both)),
        out_shape=jax.ShapeDtypeStruct((pairs.shape[0] // k, rows), jnp.float32),
        compiler_params=pltpu.CompilerParams(vmem_limit_bytes=VMEM),
        name="score",
    )(*both, *grads, pairs)


def chunks_of(hidden):
    units = hidden // TILE
    if hidden % TILE or units < 5:
        return hidden, []
    return hidden - 3 * TILE, [2 * TILE - SMALL, SMALL, TILE]


def on_device(n_dp, n_tensor, inputs, out_grad, gate_pre, down_weight, proj_in, proj_out, queries):
    rows = out_grad.shape[0]
    hidden = gate_pre.shape[1]
    me = lax.axis_index("dp")
    shard = lax.axis_index("tensor").astype(jnp.int32).reshape(1)
    far, near = n_dp // 2, 1
    ring = n_tensor <= RING
    main, spans = chunks_of(hidden)
    offsets = [main + sum(spans[:k]) for k in range(len(spans))]

    def onward(piece, hold=None):
        if hold is not None:
            piece, _ = lax.optimization_barrier((piece, hold))
        return lax.ppermute(piece, "tensor", [(i, (i + 1) % n_tensor) for i in range(n_tensor)])

    def gather(block):
        grad = lax.all_gather(block, "tensor", axis=0, tiled=False)
        return jnp.transpose(grad, (1, 0, 2, 3)).reshape(2, -1, rows)

    def spread(value, mask):
        if not ring:
            total = lax.psum(value.astype(jnp.float32), "tensor")
            return [swap(total, "dp", n_dp, mask) if mask else total]
        got = [value] if not mask else []
        for step in range(0 if mask else 1, n_tensor):
            pairs = [
                (z * n_dp + d, (z + step) % n_tensor * n_dp + (d ^ mask))
                for z in range(n_tensor)
                for d in range(n_dp)
            ]
            got.append(lax.ppermute(value, ("tensor", "dp"), pairs))
        return got

    weights = (down_weight, swap(down_weight, "dp", n_dp, near))

    cut = lambda source, offset, span: source[:, offset : offset + span]
    start_gate = cut(gate_pre, offsets[-1], spans[-1]) if spans else None
    own_blocks = split_blocks(out_grad, 0, (start_gate,) if spans else ())
    far_blocks = split_blocks(out_grad, n_dp // 2, (own_blocks,))
    if spans:
        start_gate = swap(start_gate, "dp", n_dp, far)
    far_query = swap(queries, "dp", n_dp, far)
    later_gate, _ = lax.optimization_barrier((gate_pre, own_blocks))
    parts = [cut(later_gate, 0, main)]
    parts += [cut(later_gate, offset, span) for offset, span in zip(offsets[:-1], spans)]
    far_blocks, start_gate, parts, _ = lax.optimization_barrier(
        (far_blocks, start_gate, parts, far_query)
    )
    far_start = swap(far_blocks, "dp", n_dp, far)
    own = [own_blocks, onward(own_blocks)] if ring and n_tensor > 1 else [own_blocks]
    parts, _ = lax.optimization_barrier((parts, own[-1]))
    far_gate, *last_gates = [swap(part, "dp", n_dp, far) for part in parts[: len(parts) - bool(spans)]]

    def all_pairs(hold):
        blocks, _ = lax.optimization_barrier(((queries, far_query), hold))
        blocks += tuple(swap(block, "dp", n_dp, near) for block in blocks)
        return pair_queries(blocks, (0, far, near, far ^ near), proj_in.shape[1])

    proj_out = proj_out.T
    if ring and n_tensor > 1:
        split = n_tensor // 2
        while len(own) <= split:
            own.append(onward(own[-1]))
        own_early = list(enumerate(own))[:split]
        units = hidden // TILE if hidden % TILE == 0 else 0
        halves = lambda cut: [(s, n) for s, n in ((0, cut * TILE), (cut * TILE, hidden - cut * TILE)) if n]
        own_sum, after = None, ()
        for s, span in halves(units // 3):
            (own_sum,) = project(
                shard, own_early, gate_pre, weights, proj_out, s, span, 0, s, own_sum, None, after
            )
            if s == 0:
                first_sum = own_sum
            after = (own[-1],)
        early_sum = own_sum
        pairs = all_pairs(own[1])
        others = [far_start]
        for _ in range(split - 1):
            others.append(onward(others[-1], first_sum))
        far_early = list(enumerate(others))
        (partial,) = project(
            shard, far_early, None, weights, proj_out, 0, 0, hidden, 0, None, None, (own_sum,)
        )
        while len(own) < n_tensor:
            own.append(onward(own[-1], first_sum))
        own_late = list(enumerate(own))[split:]
        after = (partial, pairs)
        for s, span in halves(units // 2):
            (own_sum,) = project(
                shard, own_late, gate_pre, weights, proj_out, s, span, 0, s, own_sum, None, after
            )
            if s == 0:
                while len(others) < n_tensor:
                    hold = own_sum if len(others) == n_tensor - 1 else early_sum
                    others.append(onward(others[-1], hold))
            after = (others[-2],)
        far_late = list(enumerate(others))[split:]
    else:
        (own_sum,) = project(
            shard, [(0, gather(own_blocks))], gate_pre, weights, proj_out, 0, hidden, 0, 0, None, None, ()
        )
        far_late, partial = [(0, gather(far_start))], None
        pairs = all_pairs(own_sum)

    input_part = lax.dot_general(
        proj_in, inputs, (((0,), (1,)), ((), ())), preferred_element_type=jnp.float32
    )
    both = jnp.concatenate([input_part, own_sum])
    both, far_gate = lax.optimization_barrier((both, far_gate))
    terms = spread(both, 0)

    if spans:
        final_gate, own_sum = lax.optimization_barrier((parts[-1], own_sum))
        last_gates.append(swap(final_gate, "dp", n_dp, far))
    far_sum, *later = project(
        shard, far_late, far_gate, weights, proj_out, 0, main, sum(spans[:-1]), 0, None, partial, (own_sum,), start_gate
    )
    if later:
        for k, gate in enumerate(last_gates):
            final = k == len(last_gates) - 1
            far_sum = finish(
                later[0],
                offsets[k] - main,
                gate,
                proj_out,
                offsets[k],
                far_sum,
                jnp.bfloat16 if final else jnp.float32,
                (),
            )
    return score(terms, spread(far_sum, far), pairs)


def solution(mesh):
    return jax.shard_map(
        functools.partial(on_device, mesh.shape["dp"], mesh.shape["tensor"]),
        mesh=mesh,
        in_specs=(
            P(("parts", "dp"), "tensor"),
            P(("parts", "dp"), None, "tensor"),
            P(("parts", "dp"), "tensor"),
            P("tensor", "dp"),
            P("tensor", None),
            P("tensor", None),
            P("tensor", "dp"),
        ),
        out_specs=P("tensor", ("parts", "dp")),
        check_vma=False,
    )
```
